32 devices in a mesh: dom: 8 (over z, x), feat: 4 (over y, core).
Axes of the slice: x: 2, y: 2, z: 4, core: 2. Of those that a mesh axis runs over, the one named last changes fastest.
Arguments:
- features: bfloat16 [768, 16384], P('feat', 'dom'), may hold values from -6 to 6
- neighbors: int32 [16, 16384], P(None, 'dom'), may hold values from 0 to 3071
- degree: int32 [16384], P('dom'), may hold values from 1 to 16
- send_rows: int32 [8, 8, 128], P('dom'), may hold values from 0 to 2047
- labels: int32 [16384], P('dom'), may hold values from 0 to 1
- w_self: bfloat16 [768, 512], replicated, may hold values from -0.21875 to 0.21875
- w_neigh: bfloat16 [768, 512], replicated, may hold values from -0.21875 to 0.21875
- bias: float32 [512], replicated, may hold values from -3 to 3
- a_self: float32 [512], replicated, may hold values from -0.5 to 0.5
- a_neigh: float32 [512], replicated, may hold values from -0.5 to 0.5
Outputs:
- logits: float32 [16384], P('dom')
- grad_self: float32 [768, 512], P('feat')
- grad_neigh: float32 [768, 512], P('feat')
The draws below stay inside these ranges and needn't reach their ends.
Inputs may be any that keep to these rules, and one draw needn't show every extreme that they name: `neighbors`: slots under 2048 are the partition's own nodes, the others nodes sent by other partitions.
All inputs are finite; a program needn't handle non-finite values.
Results may differ from the reference program's by a relative error of at most 0.012.
The reference program's roundings to bfloat16 on the way (of `aggregated` and `dpre`) count: a program that leaves them out, or rounds other values in their place, can miss the bound.
Values may be sent and summed in bfloat16 or wider, within the bound.
A program may use at most 128 MiB of HBM per device.

```python
import jax
import jax.numpy as jnp
from jax import lax

D_IN = 768
HID = 512
FAN = 16
NP = 2048
B = 128
NODES = 16384
N_DOM = 8


def place_ends(array, rng, least, high):
    longest = array.shape.index(max(array.shape))
    spots = []
    for shift in (0, 1):
        where = [jax.random.randint(jax.random.fold_in(rng, axis), (), 0, length) for axis, length in enumerate(array.shape)]
        where[longest] = (where[longest] + shift) % array.shape[longest]
        spots.append(tuple(where))
    return array.at[spots[0]].set(least).at[spots[1]].set(high)


def levels(stream_key, shape, shards, low, largest):
    def one(axis_at, parts):
        draws = jax.random.uniform(jax.random.fold_in(jax.random.fold_in(stream_key, 6), axis_at), (parts,), jnp.float32, low / len(shards), largest / len(shards))
        return jnp.repeat(jnp.exp(draws), shape[axis_at] // parts).reshape((-1,) + (1,) * (len(shape) - axis_at - 1))

    loudness = one(*shards[0])
    for cut in shards[1:]:
        loudness = loudness * one(*cut)
    return loudness


def noise(own_key, shape, spread, reach, shards=(), kind=jnp.bfloat16):
    values = spread * jax.random.normal(own_key, shape, jnp.float32)
    if shards:
        values = values * levels(own_key, shape, shards, -0.22, 0.18)
    return jnp.clip(values, -reach, reach).astype(kind)


def setup_inputs(seed: int = 0) -> dict:
    arg_keys = jax.random.split(jax.random.key(seed), 11)
    features = noise(arg_keys[0], (D_IN, NODES), 1.0, 6.0, ((0, 4), (1, 8)))
    neighbors = place_ends(jax.random.randint(arg_keys[1], (FAN, NODES), 0, NP + N_DOM * B), jax.random.fold_in(arg_keys[1], 1), 0, (NP + N_DOM * B) - 1).astype(jnp.int32)
    degree = place_ends(jax.random.randint(arg_keys[2], (NODES,), 1, FAN + 1), jax.random.fold_in(arg_keys[2], 1), 1, FAN).astype(jnp.int32)
    send_rows = place_ends(jax.random.randint(arg_keys[3], (N_DOM, N_DOM, B), 0, NP), jax.random.fold_in(arg_keys[3], 1), 0, NP - 1).astype(jnp.int32)
    labels = place_ends(jax.random.randint(arg_keys[4], (NODES,), 0, 2), jax.random.fold_in(arg_keys[4], 1), 0, 1).astype(jnp.int32)
    w_self = noise(arg_keys[5], (D_IN, HID), D_IN ** -0.5, 0.21875)
    w_neigh = noise(arg_keys[6], (D_IN, HID), D_IN ** -0.5, 0.21875)
    bias = noise(arg_keys[7], (HID,), 0.5, 3.0, (), jnp.float32)
    a_self = noise(arg_keys[8], (HID,), (HID // 4) ** -0.5, 0.5, (), jnp.float32)
    a_neigh = noise(arg_keys[9], (HID,), (HID // 4) ** -0.5, 0.5, (), jnp.float32)
    return {"features": features, "neighbors": neighbors, "degree": degree, "send_rows": send_rows, "labels": labels, "w_self": w_self, "w_neigh": w_neigh, "bias": bias, "a_self": a_self, "a_neigh": a_neigh}


def reference(features, neighbors, degree, send_rows, labels, w_self, w_neigh, bias, a_self, a_neigh):
    partitions = N_DOM

    def table_index(part_index):
        own_nodes = part_index * NP + jnp.arange(NP, dtype=jnp.int32)
        remote_nodes = jnp.arange(partitions, dtype=jnp.int32)[:, None] * NP + send_rows[:, part_index, :]
        return jnp.concatenate([own_nodes, remote_nodes.reshape(-1)]).astype(jnp.int32)

    table_global = lax.map(table_index, jnp.arange(partitions, dtype=jnp.int32))
    local_lists = neighbors.reshape(FAN, partitions, NP).transpose(1, 0, 2)
    global_lists = jax.vmap(lambda table_row, listed: table_row[listed])(table_global, local_lists)
    global_flat = global_lists.transpose(1, 0, 2).reshape(FAN, NP * partitions)
    neighbor_mask = jnp.arange(FAN)[:, None] < degree[None, :]
    inverse = 1.0 / degree.astype(jnp.float32)
    mask_parts = neighbor_mask.reshape(FAN, partitions, NP).transpose(1, 0, 2)

    def aggregate(packed):
        listed, masked, scales = packed
        summed = jnp.zeros((D_IN, NP), jnp.float32)
        for neighbor_slot in range(FAN):
            taken = features[:, listed[neighbor_slot]].astype(jnp.float32)
            summed = summed + jnp.where(masked[neighbor_slot][None, :], taken, 0.0)
        return (summed * scales[None, :]).astype(jnp.bfloat16)

    aggregated = lax.map(aggregate, (global_lists, mask_parts, inverse.reshape(partitions, NP)))
    aggregated = aggregated.transpose(1, 0, 2).reshape(D_IN, NP * partitions)
    dims = (((0,), (0,)), ((), ()))
    preact = lax.dot_general(features, w_self, dims, preferred_element_type=jnp.float32) + lax.dot_general(aggregated, w_neigh, dims, preferred_element_type=jnp.float32) + bias
    hidden = jnp.maximum(preact, 0.0)
    score_self = jnp.sum(hidden * a_self, axis=1)
    score_neigh = jnp.sum(hidden * a_neigh, axis=1)
    logits = score_self + jnp.sum(jnp.where(neighbor_mask, score_neigh[global_flat], 0.0), axis=0) * inverse
    loss_scale = float(NP * N_DOM) ** -0.5
    dlogit = (jax.nn.sigmoid(logits) - labels.astype(jnp.float32)) * loss_scale
    weighted = jnp.where(neighbor_mask, (dlogit * inverse)[None, :], 0.0)
    dneigh = jnp.zeros((NP * N_DOM,), jnp.float32).at[global_flat].add(weighted)
    dpre = jnp.where(preact > 0, dlogit[:, None] * a_self + dneigh[:, None] * a_neigh, 0.0).astype(jnp.bfloat16)
    grad_self = jnp.dot(features, dpre, preferred_element_type=jnp.float32)
    grad_neigh = jnp.dot(aggregated, dpre, preferred_element_type=jnp.float32)
    return (logits, grad_self, grad_neigh)
```

```python
import functools

import jax
import jax.numpy as jnp
from jax import lax
from jax.experimental import pallas as pl
from jax.experimental.pallas import tpu as pltpu
from jax.sharding import PartitionSpec as P

MESH = pl.DeviceIdType.MESH
BF = jnp.bfloat16
F32 = jnp.float32
NN = (((1,), (0,)), ((), ()))
NT = (((1,), (1,)), ((), ()))
TN = (((0,), (0,)), ((), ()))
GROUPS = 6
BITS = 5


def dot(a, b, dims):
    return lax.dot_general(a, b, dims, preferred_element_type=F32)


def split(row):
    wide = jnp.broadcast_to(row, (16, row.shape[1]))
    sub = lax.broadcasted_iota(jnp.int32, wide.shape, 0)
    first = wide.astype(BF).astype(F32)
    rest = wide - first
    second = rest.astype(BF).astype(F32)
    third = rest - second
    out = jnp.where(sub == 0, first, jnp.where(sub == 1, second, jnp.where(sub == 2, third, 0.0)))
    return out.astype(BF)


def total(rows):
    return jnp.sum(rows, axis=0, keepdims=True)


def kernel(
    parts, slices, reduce_here, scale,
    feat_ref, neigh_ref, degree_ref, send_ref, label_ref, ws_ref, wn_ref, bias_ref, as_ref, an_ref,
    logit_ref, gself_ref, gneigh_ref,
    hi_ref, val_ref, count_ref, pick_ref, fblk_ref, ablk_ref, agg_ref, out_ref, inc_ref, inctab_ref,
    col_ref, pre_ref, mask_ref, score_ref, srow_ref, sout_ref, sin_ref, stab_ref, wsplit_ref, slot_ref,
    gout_ref, gin_ref, back_ref, dn_ref, dl_ref, acc_ref, dpre_ref, rs_out, rs_in, ag_ref,
    feat_send, feat_recv, dom_send, dom_recv,
):
    d = lax.axis_index("dom")
    f = lax.axis_index("feat")
    cols, nodes = feat_ref.shape
    fan = neigh_ref.shape[0]
    remote = send_ref.shape[1]
    table = nodes + remote
    each = remote // parts
    block = nodes // slices
    hid = ws_ref.shape[1]
    rows = table // GROUPS
    shift = rows.bit_length() - 1

    barrier = pltpu.get_barrier_semaphore()
    for j in range(1, parts):
        pl.semaphore_signal(barrier, inc=1, device_id={"dom": lax.rem(d + j, parts)}, device_id_type=MESH)
    for j in range(1, slices):
        pl.semaphore_signal(barrier, inc=1, device_id={"feat": lax.rem(f + j, slices)}, device_id_type=MESH)
    pl.semaphore_wait(barrier, parts + slices - 2)

    sent = []

    def feat_copy(phase, j, src, dst):
        copy = pltpu.make_async_remote_copy(
            src_ref=src, dst_ref=dst, send_sem=feat_send.at[phase, j], recv_sem=feat_recv.at[phase, j],
            device_id={"feat": lax.rem(f + j, slices)}, device_id_type=MESH)
        copy.start()
        sent.append(copy)

    def dom_copy(phase, j, src, dst):
        copy = pltpu.make_async_remote_copy(
            src_ref=src, dst_ref=dst, send_sem=dom_send.at[phase, j], recv_sem=dom_recv.at[phase, j],
            device_id={"dom": lax.rem(d + j, parts)}, device_id_type=MESH)
        copy.start()
        sent.append(copy)

    def feat_wait(phase, j, dst):
        pltpu.make_async_remote_copy(
            src_ref=dst, dst_ref=dst, send_sem=feat_send.at[phase, j], recv_sem=feat_recv.at[phase, j],
            device_id={"feat": lax.rem(f + j, slices)}, device_id_type=MESH).wait_recv()

    def dom_wait(phase, j, dst):
        pltpu.make_async_remote_copy(
            src_ref=dst, dst_ref=dst, send_sem=dom_send.at[phase, j], recv_sem=dom_recv.at[phase, j],
            device_id={"dom": lax.rem(d + j, parts)}, device_id_type=MESH).wait_recv()

    def feat_peer(j):
        return lax.rem(f + j, slices)

    def feat_from(j):
        return lax.rem(f + slices - j, slices)

    def dom_peer(j):
        return lax.rem(d + j, parts)

    def dom_from(j):
        return lax.rem(d + parts - j, parts)

    def span(index):
        return pl.ds(pl.multiple_of(index * block, block), block)

    step = min(256, remote)

    def pick(i, _):
        r = pl.multiple_of(i * 256, 256)
        here = lax.broadcasted_iota(jnp.int32, (256, remote), 0) + r
        pick_ref[pl.ds(r, 256), :] = jnp.where(here == send_ref[...], 1.0, 0.0).astype(BF)
        return 0

    lax.fori_loop(0, nodes // 256, pick, 0)
    for c in range(remote // step):
        got = dot(feat_ref[...], pick_ref[:, c * step:(c + 1) * step], NN).astype(BF)
        for p in range(step // each):
            out_ref[c * (step // each) + p] = got[:, p * each:(p + 1) * each]
    for j in range(1, parts):
        dom_copy(0, j, out_ref.at[dom_peer(j)], inc_ref.at[d])
    inc_ref[d] = out_ref[d]

    for j in range(1, slices):
        feat_copy(0, j, feat_ref.at[:, span(feat_peer(j))], fblk_ref.at[f])
    fblk_ref[f] = feat_ref[:, span(f)]

    slot = lax.broadcasted_iota(jnp.int32, (fan, nodes), 0)
    used = slot < degree_ref[...]
    hi_ref[...] = neigh_ref[...] & (rows - 1)
    val_ref[...] = jnp.where(used, jnp.left_shift(jnp.int32(1), (neigh_ref[...] >> shift) * BITS), 0)

    def count_lanes(c, _):
        lanes = pl.ds(pl.multiple_of(c * 128, 128), 128)
        his = [jnp.broadcast_to(hi_ref[k:k + 1, lanes], (16, 128)) for k in range(fan)]
        vals = [jnp.broadcast_to(val_ref[k:k + 1, lanes], (16, 128)) for k in range(fan)]
        base = lax.broadcasted_iota(jnp.int32, (16, 128), 0)

        def count_rows(i, _):
            r = pl.multiple_of(i * 16, 16)
            here = base + r
            terms = [jnp.where(h == here, v, 0) for h, v in zip(his, vals)]
            while len(terms) > 1:
                terms = [a + b for a, b in zip(terms[::2], terms[1::2])] + terms[len(terms) & ~1:]
            word = terms[0]
            for g in range(GROUPS):
                part = (word >> (BITS * g)) & ((1 << BITS) - 1)
                count_ref[pl.ds(pl.multiple_of(g * rows + r, 16), 16), lanes] = part.astype(F32).astype(BF)
            return 0

        lax.fori_loop(0, rows // 16, count_rows, 0)
        return 0

    lax.fori_loop(0, nodes // 128, count_lanes, 0)
    inverse = 1.0 / degree_ref[...].astype(F32)

    for k, ref in enumerate((bias_ref, as_ref, an_ref)):
        col_ref[k] = jnp.broadcast_to(ref[...], (128, hid)).T

    for j in range(1, parts):
        dom_wait(0, j, inc_ref.at[dom_from(j)])
    for p in range(parts):
        inctab_ref[:, p * each:(p + 1) * each] = inc_ref[p]

    tile = min(256, block)

    def aggregate(index):
        for t in range(block // tile):
            lanes = pl.ds(pl.multiple_of(index * block + t * tile, tile), tile)
            sums = dot(feat_ref[...], count_ref[:nodes, lanes], NN)
            sums = sums + dot(inctab_ref[...], count_ref[nodes:, lanes], NN)
            agg_ref[:, lanes] = (sums * (1.0 / degree_ref[:, lanes].astype(F32))).astype(BF)

    def aggregate_for(j, _):
        aggregate(lax.rem(f + j, slices))
        return 0

    for j in range(1, slices):
        aggregate(feat_peer(j))
        feat_copy(1, j, agg_ref.at[:, span(feat_peer(j))], ablk_ref.at[f])
    aggregate(f)
    ablk_ref[f] = agg_ref[:, span(f)]

    for j in range(1, slices):
        feat_wait(0, j, fblk_ref.at[feat_from(j)])
    depth = slices * cols
    pre_ref[...] = dot(ws_ref[...], fblk_ref[...].reshape(depth, block), TN)
    for j in range(1, slices):
        feat_wait(1, j, ablk_ref.at[feat_from(j)])
    pre_ref[...] += dot(wn_ref[...], ablk_ref[...].reshape(depth, block), TN)
    for t in range(block // 128):
        pre = pre_ref[:, t * 128:(t + 1) * 128] + col_ref[0]
        hidden = jnp.maximum(pre, 0.0)
        mask_ref[f, :, t * 128:(t + 1) * 128] = jnp.where(pre > 0, 1.0, 0.0).astype(BF)
        own = jnp.broadcast_to(total(hidden * col_ref[1]), (8, 128))
        other = jnp.broadcast_to(total(hidden * col_ref[2]), (8, 128))
        sub = lax.broadcasted_iota(jnp.int32, (8, 128), 0)
        score_ref[f, :, t * 128:(t + 1) * 128] = jnp.where(sub == 0, own, other)
    for j in range(1, slices):
        feat_copy(2, j, score_ref.at[f], score_ref.at[f])
    for j in range(1, slices):
        feat_copy(3, j, mask_ref.at[f], mask_ref.at[f])

    for j in range(1, slices):
        feat_wait(2, j, score_ref.at[feat_from(j)])
    for s in range(slices):
        srow_ref[:, s * block:(s + 1) * block] = score_ref[s]
    boundary = total(dot(split(srow_ref[1:2, :]), pick_ref[...], NN))
    for p in range(parts):
        sout_ref[p] = jnp.broadcast_to(boundary[:, p * each:(p + 1) * each], (8, each))
    for j in range(1, parts):
        dom_copy(1, j, sout_ref.at[dom_peer(j)], sin_ref.at[d])
    sin_ref[d] = sout_ref[d]
    stab_ref[:, :nodes] = jnp.broadcast_to(srow_ref[1:2, :], (8, nodes))
    for j in range(1, parts):
        dom_wait(1, j, sin_ref.at[dom_from(j)])
    for p in range(parts):
        stab_ref[:, nodes + p * each:nodes + (p + 1) * each] = sin_ref[p]

    spread = split(stab_ref[0:1, :])

    def logit_tile(i, _):
        lanes = pl.ds(pl.multiple_of(i * 256, 256), 256)
        slot_ref[0:1, lanes] = total(dot(spread, count_ref[:, lanes], NN))
        return 0

    lax.fori_loop(0, nodes // 256, logit_tile, 0)
    logits = srow_ref[0:1, :] + slot_ref[0:1, :nodes] * inverse
    logit_ref[...] = logits
    dlogit = (1.0 / (1.0 + jnp.exp(-logits)) - label_ref[...].astype(F32)) * scale
    dl_ref[...] = dlogit
    wsplit_ref[...] = split(dlogit * inverse)

    def slot_tile(i, _):
        lanes = pl.ds(pl.multiple_of(i * 256, 256), 256)
        slot_ref[0:1, lanes] = total(dot(wsplit_ref[...], count_ref[lanes, :], NT))
        return 0

    lax.fori_loop(nodes // 256, table // 256, slot_tile, 0)
    for p in range(parts):
        gout_ref[p] = jnp.broadcast_to(slot_ref[0:1, nodes + p * each:nodes + (p + 1) * each], (8, each))
    for j in range(1, parts):
        dom_copy(2, j, gout_ref.at[dom_peer(j)], gin_ref.at[d])
    gin_ref[d] = gout_ref[d]
    lax.fori_loop(0, nodes // 256, slot_tile, 0)
    for j in range(1, parts):
        dom_wait(2, j, gin_ref.at[dom_from(j)])
    for p in range(parts):
        back_ref[:, p * each:(p + 1) * each] = gin_ref[p]
    returned = split(back_ref[0:1, :])

    def back_tile(i, _):
        lanes = pl.ds(pl.multiple_of(i * 256, 256), 256)
        dn_ref[0:1, lanes] = slot_ref[0:1, lanes] + total(dot(returned, pick_ref[lanes, :], NT))
        return 0

    lax.fori_loop(0, nodes // 256, back_tile, 0)

    for j in range(slices):
        index = feat_from(j)
        if j:
            feat_wait(3, j, mask_ref.at[index])
        for t in range(block // 128):
            lanes = pl.ds(pl.multiple_of(index * block + t * 128, 128), 128)
            grad = dl_ref[:, lanes] * col_ref[1] + dn_ref[0:1, lanes] * col_ref[2]
            keep = mask_ref[index, :, t * 128:(t + 1) * 128].astype(F32)
            dpre_ref[:, t * 128:(t + 1) * 128] = jnp.where(keep > 0, grad, 0.0).astype(BF)
        own = dot(feat_ref[:, span(index)], dpre_ref[...], NT)
        other = dot(agg_ref[:, span(index)], dpre_ref[...], NT)
        if j:
            acc_ref[:cols] += own
            acc_ref[cols:] += other
        else:
            acc_ref[:cols] = own
            acc_ref[cols:] = other

    if reduce_here:
        share = 2 * cols // parts
        for p in range(parts):
            rs_out[p] = acc_ref[p * share:(p + 1) * share].astype(BF)
        for j in range(1, parts):
            dom_copy(3, j, rs_out.at[dom_peer(j)], rs_in.at[d])
        rs_in[d] = rs_out[d]
        for j in range(1, parts):
            dom_wait(3, j, rs_in.at[dom_from(j)])
        whole = rs_in[0].astype(F32)
        for p in range(1, parts):
            whole = whole + rs_in[p].astype(F32)
        ag_ref[d] = whole.astype(BF)
        for j in range(1, parts):
            dom_copy(4, j, ag_ref.at[d], ag_ref.at[d])
        for j in range(1, parts):
            dom_wait(4, j, ag_ref.at[dom_from(j)])
        for p in range(parts):
            ref = gself_ref if p < parts // 2 else gneigh_ref
            at = (p % (parts // 2)) * share
            ref[at:at + share] = ag_ref[p].astype(F32)
    else:
        gself_ref[...] = acc_ref[:cols]
        gneigh_ref[...] = acc_ref[cols:]
    for copy in sent:
        copy.wait_send()


def body(features, neighbors, degree, send_rows, labels, w_self, w_neigh, bias, a_self, a_neigh):
    parts = lax.axis_size("dom")
    slices = lax.axis_size("feat")
    cols, nodes = features.shape
    fan = neighbors.shape[0]
    each = send_rows.shape[2]
    remote = parts * each
    table = nodes + remote
    block = nodes // slices
    hid = w_self.shape[1]
    share = 2 * cols // parts
    reduce_here = parts % 2 == 0 and share * parts == 2 * cols and share % 16 == 0
    scale = float(nodes * parts) ** (-0.5)
    spare = share if reduce_here else 16
    V = pltpu.VMEM
    scratch = [
        V((fan, nodes), jnp.int32), V((fan, nodes), jnp.int32),
        V((table, nodes), BF), V((nodes, remote), BF),
        V((slices, cols, block), BF), V((slices, cols, block), BF), V((cols, nodes), BF),
        V((parts, cols, each), BF), V((parts, cols, each), BF), V((cols, remote), BF),
        V((3, hid, 128), F32), V((hid, block), F32), V((slices, hid, block), BF),
        V((slices, 8, block), F32), V((8, nodes), F32),
        V((parts, 8, each), F32), V((parts, 8, each), F32), V((8, table), F32),
        V((16, nodes), BF), V((8, table), F32),
        V((parts, 8, each), F32), V((parts, 8, each), F32), V((8, remote), F32),
        V((8, nodes), F32), V((1, nodes), F32),
        V((2 * cols, hid), F32), V((hid, block), BF),
        V((parts, spare, hid), BF), V((parts, spare, hid), BF), V((parts, spare, hid), BF),
        pltpu.SemaphoreType.DMA((4, slices)), pltpu.SemaphoreType.DMA((4, slices)),
        pltpu.SemaphoreType.DMA((5, parts)), pltpu.SemaphoreType.DMA((5, parts)),
    ]
    vm = pl.BlockSpec(memory_space=pltpu.VMEM)
    logits, grad_self, grad_neigh = pl.pallas_call(
        functools.partial(kernel, parts, slices, reduce_here, scale),
        out_shape=(
            jax.ShapeDtypeStruct((1, nodes), F32),
            jax.ShapeDtypeStruct((cols, hid), F32),
            jax.ShapeDtypeStruct((cols, hid), F32),
        ),
        in_specs=[vm] * 10,
        out_specs=(vm, vm, vm),
        scratch_shapes=scratch,
        compiler_params=pltpu.CompilerParams(
            collective_id=0, has_side_effects=True, vmem_limit_bytes=52 * 1024 * 1024),
    )(
        features, neighbors, degree.reshape(1, nodes), send_rows.reshape(1, remote), labels.reshape(1, nodes),
        w_self, w_neigh, bias.reshape(1, hid), a_self.reshape(1, hid), a_neigh.reshape(1, hid),
    )
    if not reduce_here:
        grad_self, grad_neigh = lax.psum((grad_self, grad_neigh), "dom")
    return (logits.reshape(nodes), grad_self, grad_neigh)


def solution(mesh):
    return jax.shard_map(
        body,
        mesh=mesh,
        in_specs=(
            P("feat", "dom"), P(None, "dom"), P("dom"), P("dom", None, None), P("dom"),
            P(), P(), P(), P(), P(),
        ),
        out_specs=(P("dom"), P("feat", None), P("feat", None)),
        check_vma=False,
    )
```

```python
import functools

import jax
import jax.numpy as jnp
from jax import lax
from jax.experimental import pallas as pl
from jax.experimental.pallas import tpu as pltpu
from jax.sharding import PartitionSpec as P

MESH = pl.DeviceIdType.MESH
BF = jnp.bfloat16
F32 = jnp.float32
NN = (((1,), (0,)), ((), ()))
NT = (((1,), (1,)), ((), ()))
TN = (((0,), (0,)), ((), ()))
GROUPS = 6
BITS = 5


def dot(a, b, dims):
    return lax.dot_general(a, b, dims, preferred_element_type=F32)


def split(row):
    wide = jnp.broadcast_to(row, (16, row.shape[1]))
    sub = lax.broadcasted_iota(jnp.int32, wide.shape, 0)
    first = wide.astype(BF).astype(F32)
    rest = wide - first
    second = rest.astype(BF).astype(F32)
    third = rest - second
    out = jnp.where(sub == 0, first, jnp.where(sub == 1, second, jnp.where(sub == 2, third, 0.0)))
    return out.astype(BF)


def total(rows):
    return jnp.sum(rows, axis=0, keepdims=True)


def kernel(
    parts, slices, reduce_here, scale,
    *refs,
):
    inputs, refs = refs[:10], refs[10:]
    held, refs = refs[3:13], refs[:3] + refs[13:]
    run(parts, slices, reduce_here, scale, inputs, held, *refs)


def run(
    parts, slices, reduce_here, scale, inputs, held,
    logit_ref, gself_ref, gneigh_ref,
    hi_ref, val_ref, count_ref, pick_ref, fblk_ref, ablk_ref, agg_ref, out_ref, inc_ref, inctab_ref,
    col_ref, pre_ref, mask_ref, score_ref, srow_ref, sout_ref, sin_ref, stab_ref, wsplit_ref, slot_ref,
    gout_ref, gin_ref, back_ref, dn_ref, dl_ref, acc_ref, dpre_ref, rs_out, rs_in, ag_ref,
    feat_send, feat_recv, dom_send, dom_recv, load_sem,
):
    feat_ref, neigh_ref, degree_ref, send_ref, label_ref, ws_ref, wn_ref, bias_ref, as_ref, an_ref = held
    loads = [pltpu.make_async_copy(a, b, load_sem.at[k]) for k, (a, b) in enumerate(zip(inputs, held))]
    for k in (0, 3, 1, 2, 5, 7, 8, 9, 6, 4):
        loads[k].start()
    d = lax.axis_index("dom")
    f = lax.axis_index("feat")
    cols, nodes = feat_ref.shape
    fan = neigh_ref.shape[0]
    each = send_ref.shape[1]
    remote = parts * each
    table = nodes + remote
    block = nodes // slices
    hid = ws_ref.shape[1]
    rows = table // GROUPS
    shift = rows.bit_length() - 1

    chips = slices // 2
    chip, core = f // 2, lax.rem(f, 2)

    def feat_peer(j):
        return 2 * lax.rem(chip + j // 2, chips) + lax.rem(core + j % 2, 2)

    def feat_from(j):
        return 2 * lax.rem(chip + chips - j // 2, chips) + lax.rem(core + j % 2, 2)

    far_first = list(range(2, slices)) + [1]

    barrier = pltpu.get_barrier_semaphore()
    for j in range(1, parts):
        pl.semaphore_signal(barrier, inc=1, device_id={"dom": lax.rem(d + j, parts)}, device_id_type=MESH)
    for j in range(1, slices):
        pl.semaphore_signal(barrier, inc=1, device_id={"feat": feat_peer(j)}, device_id_type=MESH)
    pl.semaphore_wait(barrier, parts + slices - 2)

    sent = []

    def feat_copy(phase, j, src, dst):
        copy = pltpu.make_async_remote_copy(
            src_ref=src, dst_ref=dst, send_sem=feat_send.at[phase, j], recv_sem=feat_recv.at[phase, j],
            device_id={"feat": feat_peer(j)}, device_id_type=MESH)
        copy.start()
        sent.append(copy)

    def dom_copy(phase, j, src, dst):
        copy = pltpu.make_async_remote_copy(
            src_ref=src, dst_ref=dst, send_sem=dom_send.at[phase, j], recv_sem=dom_recv.at[phase, j],
            device_id={"dom": lax.rem(d + j, parts)}, device_id_type=MESH)
        copy.start()
        sent.append(copy)

    def forward(phase, j, src, dst):
        copy = pltpu.make_async_remote_copy(
            src_ref=src, dst_ref=dst, send_sem=feat_send.at[phase, j], recv_sem=feat_recv.at[phase, j],
            device_id={"feat": feat_peer(1)}, device_id_type=MESH)
        copy.start()
        sent.append(copy)

    def feat_wait(phase, j, dst):
        pltpu.make_async_remote_copy(
            src_ref=dst, dst_ref=dst, send_sem=feat_send.at[phase, j], recv_sem=feat_recv.at[phase, j],
            device_id={"feat": feat_peer(j)}, device_id_type=MESH).wait_recv()

    def dom_wait(phase, j, dst):
        pltpu.make_async_remote_copy(
            src_ref=dst, dst_ref=dst, send_sem=dom_send.at[phase, j], recv_sem=dom_recv.at[phase, j],
            device_id={"dom": lax.rem(d + j, parts)}, device_id_type=MESH).wait_recv()

    def dom_peer(j):
        return lax.rem(d + j, parts)

    def dom_from(j):
        return lax.rem(d + parts - j, parts)

    def span(index):
        return pl.ds(pl.multiple_of(index * block, block), block)

    loads[0].wait()
    loads[3].wait()

    def pick(p, lanes):
        def pick_rows(i, _):
            r = pl.multiple_of(i * 256, 256)
            here = lax.broadcasted_iota(jnp.int32, (256, each), 0) + r
            pick_ref[pl.ds(r, 256), lanes] = jnp.where(here == send_ref[pl.ds(p, 1), :], 1.0, 0.0).astype(BF)
            return 0

        lax.fori_loop(0, nodes // 256, pick_rows, 0)
        out_ref[p] = dot(feat_ref[...], pick_ref[:, lanes], NN).astype(BF)

    if each % 128 == 0:
        for j in list(range(1, parts)) + [0]:
            p = dom_peer(j)
            pick(p, pl.ds(pl.multiple_of(p * each, 128), each))
            if j:
                dom_copy(0, j, out_ref.at[p], inc_ref.at[d])
    else:
        for p in range(parts):
            pick(p, slice(p * each, (p + 1) * each))
        for j in range(1, parts):
            dom_copy(0, j, out_ref.at[dom_peer(j)], inc_ref.at[d])
    inc_ref[d] = out_ref[d]

    for j in far_first:
        feat_copy(0, j, feat_ref.at[:, span(feat_peer(j))], fblk_ref.at[f])
    fblk_ref[f] = feat_ref[:, span(f)]

    loads[1].wait()
    loads[2].wait()
    slot = lax.broadcasted_iota(jnp.int32, (fan, nodes), 0)
    used = slot < degree_ref[...]
    hi_ref[...] = neigh_ref[...] & (rows - 1)
    val_ref[...] = jnp.where(used, jnp.left_shift(jnp.int32(1), (neigh_ref[...] >> shift) * BITS), 0)

    def count_lanes(c, first):
        lanes = pl.ds(pl.multiple_of(first + c * 128, 128), 128)
        his = [jnp.broadcast_to(hi_ref[k:k + 1, lanes], (16, 128)) for k in range(fan)]
        vals = [jnp.broadcast_to(val_ref[k:k + 1, lanes], (16, 128)) for k in range(fan)]
        base = lax.broadcasted_iota(jnp.int32, (16, 128), 0)

        def count_rows(i, _):
            r = pl.multiple_of(i * 16, 16)
            here = base + r
            terms = [jnp.where(h == here, v, 0) for h, v in zip(his, vals)]
            while len(terms) > 1:
                terms = [a + b for a, b in zip(terms[::2], terms[1::2])] + terms[len(terms) & ~1:]
            word = terms[0]
            for g in range(GROUPS):
                part = (word >> (BITS * g)) & ((1 << BITS) - 1)
                count_ref[pl.ds(pl.multiple_of(g * rows + r, 16), 16), lanes] = part.astype(F32).astype(BF)
            return 0

        lax.fori_loop(0, rows // 16, count_rows, 0)
        return first

    def count_block(index):
        lax.fori_loop(0, block // 128, count_lanes, index * block)

    for j in far_first:
        count_block(feat_peer(j))
    inverse = 1.0 / degree_ref[...].astype(F32)

    for k in (7, 8, 9):
        loads[k].wait()
    for k, ref in enumerate((bias_ref, as_ref, an_ref)):
        col_ref[k] = jnp.broadcast_to(ref[...], (128, hid)).T

    for j in range(1, parts):
        dom_wait(0, j, inc_ref.at[dom_from(j)])
    for p in range(parts):
        inctab_ref[:, p * each:(p + 1) * each] = inc_ref[p]

    tile = min(256, block)

    def aggregate(index):
        for t in range(block // tile):
            lanes = pl.ds(pl.multiple_of(index * block + t * tile, tile), tile)
            sums = dot(feat_ref[...], count_ref[:nodes, lanes], NN)
            sums = sums + dot(inctab_ref[...], count_ref[nodes:, lanes], NN)
            agg_ref[:, lanes] = (sums * (1.0 / degree_ref[:, lanes].astype(F32))).astype(BF)

    for j in far_first:
        aggregate(feat_peer(j))
        feat_copy(1, j, agg_ref.at[:, span(feat_peer(j))], ablk_ref.at[f])
    count_block(f)
    aggregate(f)
    ablk_ref[f] = agg_ref[:, span(f)]

    for j in range(1, slices):
        feat_wait(0, j, fblk_ref.at[feat_from(j)])
    depth = slices * cols
    loads[5].wait()
    pre_ref[...] = dot(ws_ref[...], fblk_ref[...].reshape(depth, block), TN)
    for j in range(1, slices):
        feat_wait(1, j, ablk_ref.at[feat_from(j)])
    loads[6].wait()
    pre_ref[...] += dot(wn_ref[...], ablk_ref[...].reshape(depth, block), TN)
    for t in range(block // 128):
        pre = pre_ref[:, t * 128:(t + 1) * 128] + col_ref[0]
        hidden = jnp.maximum(pre, 0.0)
        mask_ref[f, :, t * 128:(t + 1) * 128] = jnp.where(pre > 0, 1.0, 0.0).astype(BF)
        own = jnp.broadcast_to(total(hidden * col_ref[1]), (8, 128))
        other = jnp.broadcast_to(total(hidden * col_ref[2]), (8, 128))
        sub = lax.broadcasted_iota(jnp.int32, (8, 128), 0)
        score_ref[f, :, t * 128:(t + 1) * 128] = jnp.where(sub == 0, own, other)
    for j in far_first:
        feat_copy(2, j, score_ref.at[f], score_ref.at[f])
    for j in range(2, slices, 2):
        feat_copy(3, j, mask_ref.at[f], mask_ref.at[f])
    feat_copy(3, 1, mask_ref.at[f], mask_ref.at[f])

    for j in range(1, slices):
        feat_wait(2, j, score_ref.at[feat_from(j)])
    for s in range(slices):
        srow_ref[:, s * block:(s + 1) * block] = score_ref[s]
    own_score = split(srow_ref[1:2, :])
    boundary = total(dot(own_score, pick_ref[...], NN))
    for p in range(parts):
        sout_ref[p] = jnp.broadcast_to(boundary[:, p * each:(p + 1) * each], (8, each))
    for j in range(1, parts):
        dom_copy(1, j, sout_ref.at[dom_peer(j)], sin_ref.at[d])
    sin_ref[d] = sout_ref[d]

    def own_tile(i, _):
        lanes = pl.ds(pl.multiple_of(i * 256, 256), 256)
        slot_ref[0:1, lanes] = total(dot(own_score, count_ref[:nodes, lanes], NN))
        return 0

    lax.fori_loop(0, nodes // 256, own_tile, 0)
    for j in range(1, parts):
        dom_wait(1, j, sin_ref.at[dom_from(j)])
    for p in range(parts):
        stab_ref[:, p * each:(p + 1) * each] = sin_ref[p]
    spread = split(stab_ref[0:1, :])

    def logit_tile(i, _):
        lanes = pl.ds(pl.multiple_of(i * 256, 256), 256)
        slot_ref[0:1, lanes] += total(dot(spread, count_ref[nodes:, lanes], NN))
        return 0

    lax.fori_loop(0, nodes // 256, logit_tile, 0)
    logits = srow_ref[0:1, :] + slot_ref[0:1, :nodes] * inverse
    logit_ref[...] = logits
    loads[4].wait()
    dlogit = (1.0 / (1.0 + jnp.exp(-logits)) - label_ref[...].astype(F32)) * scale
    dl_ref[...] = dlogit
    wsplit_ref[...] = split(dlogit * inverse)

    for j in range(2, slices, 2):
        feat_wait(3, j, mask_ref.at[feat_from(j)])
        index = feat_from(j)
        forward(3, j + 1, mask_ref.at[index], mask_ref.at[index])

    def slot_tile(i, _):
        lanes = pl.ds(pl.multiple_of(i * 256, 256), 256)
        slot_ref[0:1, lanes] = total(dot(wsplit_ref[...], count_ref[lanes, :], NT))
        return 0

    lax.fori_loop(nodes // 256, table // 256, slot_tile, 0)
    for p in range(parts):
        gout_ref[p] = jnp.broadcast_to(slot_ref[0:1, nodes + p * each:nodes + (p + 1) * each], (8, each))
    for j in range(1, parts):
        dom_copy(2, j, gout_ref.at[dom_peer(j)], gin_ref.at[d])
    gin_ref[d] = gout_ref[d]
    lax.fori_loop(0, nodes // 256, slot_tile, 0)
    for j in range(1, parts):
        dom_wait(2, j, gin_ref.at[dom_from(j)])
    for p in range(parts):
        back_ref[:, p * each:(p + 1) * each] = gin_ref[p]
    returned = split(back_ref[0:1, :])

    def back_tile(i, _):
        lanes = pl.ds(pl.multiple_of(i * 256, 256), 256)
        dn_ref[0:1, lanes] = slot_ref[0:1, lanes] + total(dot(returned, pick_ref[lanes, :], NT))
        return 0

    lax.fori_loop(0, nodes // 256, back_tile, 0)

    for j in range(slices):
        index = feat_from(j)
        if j % 2:
            feat_wait(3, j, mask_ref.at[index])
        for t in range(block // 128):
            lanes = pl.ds(pl.multiple_of(index * block + t * 128, 128), 128)
            grad = dl_ref[:, lanes] * col_ref[1] + dn_ref[0:1, lanes] * col_ref[2]
            keep = mask_ref[index, :, t * 128:(t + 1) * 128].astype(F32)
            dpre_ref[:, t * 128:(t + 1) * 128] = jnp.where(keep > 0, grad, 0.0).astype(BF)
        own = dot(feat_ref[:, span(index)], dpre_ref[...], NT)
        other = dot(agg_ref[:, span(index)], dpre_ref[...], NT)
        if j:
            acc_ref[:cols] += own
            acc_ref[cols:] += other
        else:
            acc_ref[:cols] = own
            acc_ref[cols:] = other

    if reduce_here:
        share = 2 * cols // parts
        for p in range(parts):
            rs_out[p] = acc_ref[p * share:(p + 1) * share].astype(BF)
        for j in range(1, parts):
            dom_copy(3, j, rs_out.at[dom_peer(j)], rs_in.at[d])
        rs_in[d] = rs_out[d]
        for j in range(1, parts):
            dom_wait(3, j, rs_in.at[dom_from(j)])
        whole = rs_in[0].astype(F32)
        for p in range(1, parts):
            whole = whole + rs_in[p].astype(F32)
        ag_ref[d] = whole.astype(BF)
        for j in range(1, parts):
            dom_copy(4, j, ag_ref.at[d], ag_ref.at[d])
        for j in range(1, parts):
            dom_wait(4, j, ag_ref.at[dom_from(j)])
        for p in range(parts):
            ref = gself_ref if p < parts // 2 else gneigh_ref
            at = (p % (parts // 2)) * share
            ref[at:at + share] = ag_ref[p].astype(F32)
    else:
        gself_ref[...] = acc_ref[:cols]
        gneigh_ref[...] = acc_ref[cols:]
    for copy in sent:
        copy.wait_send()


def body(features, neighbors, degree, send_rows, labels, w_self, w_neigh, bias, a_self, a_neigh):
    parts = lax.axis_size("dom")
    slices = lax.axis_size("feat")
    cols, nodes = features.shape
    fan = neighbors.shape[0]
    each = send_rows.shape[2]
    remote = parts * each
    table = nodes + remote
    block = nodes // slices
    hid = w_self.shape[1]
    share = 2 * cols // parts
    reduce_here = parts % 2 == 0 and share * parts == 2 * cols and share % 16 == 0
    scale = float(nodes * parts) ** (-0.5)
    spare = share if reduce_here else 16
    V = pltpu.VMEM
    held = [
        V((cols, nodes), BF), V((fan, nodes), jnp.int32), V((1, nodes), jnp.int32), V((parts, each), jnp.int32),
        V((1, nodes), jnp.int32), V(w_self.shape, BF), V(w_neigh.shape, BF),
        V((1, hid), F32), V((1, hid), F32), V((1, hid), F32),
    ]
    scratch = held + [
        V((fan, nodes), jnp.int32), V((fan, nodes), jnp.int32),
        V((table, nodes), BF), V((nodes, remote), BF),
        V((slices, cols, block), BF), V((slices, cols, block), BF), V((cols, nodes), BF),
        V((parts, cols, each), BF), V((parts, cols, each), BF), V((cols, remote), BF),
        V((3, hid, 128), F32), V((hid, block), F32), V((slices, hid, block), BF),
        V((slices, 8, block), F32), V((8, nodes), F32),
        V((parts, 8, each), F32), V((parts, 8, each), F32), V((8, remote), F32),
        V((16, nodes), BF), V((8, table), F32),
        V((parts, 8, each), F32), V((parts, 8, each), F32), V((8, remote), F32),
        V((8, nodes), F32), V((1, nodes), F32),
        V((2 * cols, hid), F32), V((hid, block), BF),
        V((parts, spare, hid), BF), V((parts, spare, hid), BF), V((parts, spare, hid), BF),
        pltpu.SemaphoreType.DMA((4, slices)), pltpu.SemaphoreType.DMA((4, slices)),
        pltpu.SemaphoreType.DMA((5, parts)), pltpu.SemaphoreType.DMA((5, parts)),
        pltpu.SemaphoreType.DMA((10,)),
    ]
    vm = pl.BlockSpec(memory_space=pltpu.VMEM)
    logits, grad_self, grad_neigh = pl.pallas_call(
        functools.partial(kernel, parts, slices, reduce_here, scale),
        out_shape=(
            jax.ShapeDtypeStruct((1, nodes), F32),
            jax.ShapeDtypeStruct((cols, hid), F32),
            jax.ShapeDtypeStruct((cols, hid), F32),
        ),
        in_specs=[pl.BlockSpec(memory_space=pltpu.HBM)] * 10,
        out_specs=(vm, vm, vm),
        scratch_shapes=scratch,
        compiler_params=pltpu.CompilerParams(
            collective_id=0, has_side_effects=True, vmem_limit_bytes=52 * 1024 * 1024),
    )(
        features, neighbors, degree.reshape(1, nodes), send_rows.reshape(parts, each), labels.reshape(1, nodes),
        w_self, w_neigh, bias.reshape(1, hid), a_self.reshape(1, hid), a_neigh.reshape(1, hid),
    )
    if not reduce_here:
        grad_self, grad_neigh = lax.psum((grad_self, grad_neigh), "dom")
    return (logits.reshape(nodes), grad_self, grad_neigh)


def solution(mesh):
    return jax.shard_map(
        body,
        mesh=mesh,
        in_specs=(
            P("feat", "dom"), P(None, "dom"), P("dom"), P("dom", None, None), P("dom"),
            P(), P(), P(), P(), P(),
        ),
        out_specs=(P("dom"), P("feat", None), P("feat", None)),
        check_vma=False,
    )
```

```python
import functools

import jax
import jax.numpy as jnp
from jax import lax
from jax.experimental import pallas as pl
from jax.experimental.pallas import tpu as pltpu
from jax.sharding import PartitionSpec as P

MESH = pl.DeviceIdType.MESH
BF = jnp.bfloat16
F32 = jnp.float32
NN = (((1,), (0,)), ((), ()))
NT = (((1,), (1,)), ((), ()))
TN = (((0,), (0,)), ((), ()))
GROUPS = 6
BITS = 5


def dot(a, b, dims):
    return lax.dot_general(a, b, dims, preferred_element_type=F32)


def split(row):
    wide = jnp.broadcast_to(row, (16, row.shape[1]))
    sub = lax.broadcasted_iota(jnp.int32, wide.shape, 0)
    first = wide.astype(BF).astype(F32)
    rest = wide - first
    second = rest.astype(BF).astype(F32)
    third = rest - second
    out = jnp.where(sub == 0, first, jnp.where(sub == 1, second, jnp.where(sub == 2, third, 0.0)))
    return out.astype(BF)


def total(rows):
    return jnp.sum(rows, axis=0, keepdims=True)


def kernel(
    parts, slices, reduce_here, scale,
    *refs,
):
    inputs, refs = refs[:10], refs[10:]
    held, refs = refs[3:13], refs[:3] + refs[13:]
    run(parts, slices, reduce_here, scale, inputs, held, *refs)


def run(
    parts, slices, reduce_here, scale, inputs, held,
    logit_ref, gself_ref, gneigh_ref,
    hi_ref, val_ref, count_ref, pick_ref, fblk_ref, ablk_ref, agg_ref, out_ref, inc_ref, inctab_ref,
    col_ref, pre_ref, mask_ref, score_ref, srow_ref, sout_ref, sin_ref, stab_ref, wsplit_ref, slot_ref,
    gout_ref, gin_ref, back_ref, dn_ref, dl_ref, acc_ref, dpre_ref, rs_out, rs_in, ag_ref,
    feat_send, feat_recv, dom_send, dom_recv, load_sem,
):
    feat_ref, neigh_ref, degree_ref, send_ref, label_ref, ws_ref, wn_ref, bias_ref, as_ref, an_ref = held
    loads = [pltpu.make_async_copy(a, b, load_sem.at[k]) for k, (a, b) in enumerate(zip(inputs, held))]
    for k in (0, 3, 1, 2, 5, 7, 8, 9, 6, 4):
        loads[k].start()
    d = lax.axis_index("dom")
    f = lax.axis_index("feat")
    cols, nodes = feat_ref.shape
    fan = neigh_ref.shape[0]
    each = send_ref.shape[1]
    remote = parts * each
    table = nodes + remote
    block = nodes // slices
    hid = ws_ref.shape[1]
    rows = table // GROUPS
    shift = rows.bit_length() - 1

    chips = slices // 2
    chip, core = f // 2, lax.rem(f, 2)

    def feat_peer(j):
        return 2 * lax.rem(chip + j // 2, chips) + lax.rem(core + j % 2, 2)

    def feat_from(j):
        return 2 * lax.rem(chip + chips - j // 2, chips) + lax.rem(core + j % 2, 2)

    far_first = list(range(2, slices)) + [1]

    barrier = pltpu.get_barrier_semaphore()
    for j in range(1, parts):
        pl.semaphore_signal(barrier, inc=1, device_id={"dom": lax.rem(d + j, parts)}, device_id_type=MESH)
    for j in range(1, slices):
        pl.semaphore_signal(barrier, inc=1, device_id={"feat": feat_peer(j)}, device_id_type=MESH)
    pl.semaphore_wait(barrier, parts + slices - 2)

    sent = []

    def feat_copy(phase, j, src, dst):
        copy = pltpu.make_async_remote_copy(
            src_ref=src, dst_ref=dst, send_sem=feat_send.at[phase, j], recv_sem=feat_recv.at[phase, j],
            device_id={"feat": feat_peer(j)}, device_id_type=MESH)
        copy.start()
        sent.append(copy)

    def dom_copy(phase, j, src, dst):
        copy = pltpu.make_async_remote_copy(
            src_ref=src, dst_ref=dst, send_sem=dom_send.at[phase, j], recv_sem=dom_recv.at[phase, j],
            device_id={"dom": lax.rem(d + j, parts)}, device_id_type=MESH)
        copy.start()
        sent.append(copy)

    def forward(phase, j, src, dst):
        copy = pltpu.make_async_remote_copy(
            src_ref=src, dst_ref=dst, send_sem=feat_send.at[phase, j], recv_sem=feat_recv.at[phase, j],
            device_id={"feat": feat_peer(1)}, device_id_type=MESH)
        copy.start()
        sent.append(copy)

    def feat_wait(phase, j, dst):
        pltpu.make_async_remote_copy(
            src_ref=dst, dst_ref=dst, send_sem=feat_send.at[phase, j], recv_sem=feat_recv.at[phase, j],
            device_id={"feat": feat_peer(j)}, device_id_type=MESH).wait_recv()

    def dom_wait(phase, j, dst):
        pltpu.make_async_remote_copy(
            src_ref=dst, dst_ref=dst, send_sem=dom_send.at[phase, j], recv_sem=dom_recv.at[phase, j],
            device_id={"dom": lax.rem(d + j, parts)}, device_id_type=MESH).wait_recv()

    def dom_peer(j):
        return lax.rem(d + j, parts)

    def dom_from(j):
        return lax.rem(d + parts - j, parts)

    def span(index):
        return pl.ds(pl.multiple_of(index * block, block), block)

    loads[0].wait()
    loads[3].wait()

    def pick(i, _):
        r = pl.multiple_of(i * 256, 256)
        here = lax.broadcasted_iota(jnp.int32, (256, each), 0) + r
        for p in range(parts):
            pick_ref[pl.ds(r, 256), p * each:(p + 1) * each] = jnp.where(here == send_ref[p:p + 1, :], 1.0, 0.0).astype(BF)
        return 0

    lax.fori_loop(0, nodes // 256, pick, 0)
    step = min(256, remote)
    for c in range(remote // step):
        got = dot(feat_ref[...], pick_ref[:, c * step:(c + 1) * step], NN).astype(BF)
        for p in range(step // each):
            out_ref[c * (step // each) + p] = got[:, p * each:(p + 1) * each]
    for j in range(1, parts):
        dom_copy(0, j, out_ref.at[dom_peer(j)], inc_ref.at[d])
    inc_ref[d] = out_ref[d]

    for j in far_first:
        feat_copy(0, j, feat_ref.at[:, span(feat_peer(j))], fblk_ref.at[f])
    fblk_ref[f] = feat_ref[:, span(f)]

    loads[1].wait()
    loads[2].wait()
    slot = lax.broadcasted_iota(jnp.int32, (fan, nodes), 0)
    used = slot < degree_ref[...]
    hi_ref[...] = neigh_ref[...] & (rows - 1)
    val_ref[...] = jnp.where(used, jnp.left_shift(jnp.int32(1), (neigh_ref[...] >> shift) * BITS), 0)

    def count_lanes(c, first):
        lanes = pl.ds(pl.multiple_of(first + c * 128, 128), 128)
        his = [jnp.broadcast_to(hi_ref[k:k + 1, lanes], (16, 128)) for k in range(fan)]
        vals = [jnp.broadcast_to(val_ref[k:k + 1, lanes], (16, 128)) for k in range(fan)]
        base = lax.broadcasted_iota(jnp.int32, (16, 128), 0)

        def count_rows(i, _):
            r = pl.multiple_of(i * 16, 16)
            here = base + r
            terms = [jnp.where(h == here, v, 0) for h, v in zip(his, vals)]
            while len(terms) > 1:
                terms = [a + b for a, b in zip(terms[::2], terms[1::2])] + terms[len(terms) & ~1:]
            word = terms[0]
            for g in range(GROUPS):
                part = (word >> (BITS * g)) & ((1 << BITS) - 1)
                count_ref[pl.ds(pl.multiple_of(g * rows + r, 16), 16), lanes] = part.astype(F32).astype(BF)
            return 0

        lax.fori_loop(0, rows // 16, count_rows, 0)
        return first

    def count_block(index):
        lax.fori_loop(0, block // 128, count_lanes, index * block)

    for j in far_first:
        count_block(feat_peer(j))
    inverse = 1.0 / degree_ref[...].astype(F32)

    for k in (7, 8, 9):
        loads[k].wait()
    for k, ref in enumerate((bias_ref, as_ref, an_ref)):
        col_ref[k] = jnp.broadcast_to(ref[...], (128, hid)).T

    for j in range(1, parts):
        dom_wait(0, j, inc_ref.at[dom_from(j)])
    for p in range(parts):
        inctab_ref[:, p * each:(p + 1) * each] = inc_ref[p]

    tile = min(256, block)

    def aggregate(index):
        for t in range(block // tile):
            lanes = pl.ds(pl.multiple_of(index * block + t * tile, tile), tile)
            sums = dot(feat_ref[...], count_ref[:nodes, lanes], NN)
            sums = sums + dot(inctab_ref[...], count_ref[nodes:, lanes], NN)
            agg_ref[:, lanes] = (sums * (1.0 / degree_ref[:, lanes].astype(F32))).astype(BF)

    for j in far_first:
        aggregate(feat_peer(j))
        feat_copy(1, j, agg_ref.at[:, span(feat_peer(j))], ablk_ref.at[f])
    count_block(f)
    aggregate(f)
    ablk_ref[f] = agg_ref[:, span(f)]

    for j in range(1, slices):
        feat_wait(0, j, fblk_ref.at[feat_from(j)])
    depth = slices * cols
    loads[5].wait()
    pre_ref[...] = dot(ws_ref[...], fblk_ref[...].reshape(depth, block), TN)
    for j in range(1, slices):
        feat_wait(1, j, ablk_ref.at[feat_from(j)])
    loads[6].wait()
    pre_ref[...] += dot(wn_ref[...], ablk_ref[...].reshape(depth, block), TN)
    for t in range(block // 128):
        pre = pre_ref[:, t * 128:(t + 1) * 128] + col_ref[0]
        hidden = jnp.maximum(pre, 0.0)
        mask_ref[f, :, t * 128:(t + 1) * 128] = jnp.where(pre > 0, 1.0, 0.0).astype(BF)
        own = jnp.broadcast_to(total(hidden * col_ref[1]), (8, 128))
        other = jnp.broadcast_to(total(hidden * col_ref[2]), (8, 128))
        sub = lax.broadcasted_iota(jnp.int32, (8, 128), 0)
        score_ref[f, :, t * 128:(t + 1) * 128] = jnp.where(sub == 0, own, other)
    for j in far_first:
        feat_copy(2, j, score_ref.at[f], score_ref.at[f])
    for j in range(2, slices, 2):
        feat_copy(3, j, mask_ref.at[f], mask_ref.at[f])
    feat_copy(3, 1, mask_ref.at[f], mask_ref.at[f])

    for j in range(1, slices):
        feat_wait(2, j, score_ref.at[feat_from(j)])
    for s in range(slices):
        srow_ref[:, s * block:(s + 1) * block] = score_ref[s]
    own_score = split(srow_ref[1:2, :])
    boundary = total(dot(own_score, pick_ref[...], NN))
    for p in range(parts):
        sout_ref[p] = jnp.broadcast_to(boundary[:, p * each:(p + 1) * each], (8, each))
    for j in range(1, parts):
        dom_copy(1, j, sout_ref.at[dom_peer(j)], sin_ref.at[d])
    sin_ref[d] = sout_ref[d]

    def own_tile(i, _):
        lanes = pl.ds(pl.multiple_of(i * 256, 256), 256)
        slot_ref[0:1, lanes] = total(dot(own_score, count_ref[:nodes, lanes], NN))
        return 0

    lax.fori_loop(0, nodes // 256, own_tile, 0)
    for j in range(1, parts):
        dom_wait(1, j, sin_ref.at[dom_from(j)])
    for p in range(parts):
        stab_ref[:, p * each:(p + 1) * each] = sin_ref[p]
    spread = split(stab_ref[0:1, :])

    def logit_tile(i, _):
        lanes = pl.ds(pl.multiple_of(i * 256, 256), 256)
        slot_ref[0:1, lanes] += total(dot(spread, count_ref[nodes:, lanes], NN))
        return 0

    lax.fori_loop(0, nodes // 256, logit_tile, 0)
    logits = srow_ref[0:1, :] + slot_ref[0:1, :nodes] * inverse
    logit_ref[...] = logits
    loads[4].wait()
    dlogit = (1.0 / (1.0 + jnp.exp(-logits)) - label_ref[...].astype(F32)) * scale
    dl_ref[...] = dlogit
    wsplit_ref[...] = split(dlogit * inverse)

    def slot_tile(i, _):
        lanes = pl.ds(pl.multiple_of(i * 256, 256), 256)
        slot_ref[0:1, lanes] = total(dot(wsplit_ref[...], count_ref[lanes, :], NT))
        return 0

    lax.fori_loop(nodes // 256, table // 256, slot_tile, 0)
    for p in range(parts):
        gout_ref[p] = jnp.broadcast_to(slot_ref[0:1, nodes + p * each:nodes + (p + 1) * each], (8, each))
    for j in range(1, parts):
        dom_copy(2, j, gout_ref.at[dom_peer(j)], gin_ref.at[d])
    gin_ref[d] = gout_ref[d]
    lax.fori_loop(0, nodes // 256, slot_tile, 0)

    for j in range(2, slices, 2):
        feat_wait(3, j, mask_ref.at[feat_from(j)])
        index = feat_from(j)
        forward(3, j + 1, mask_ref.at[index], mask_ref.at[index])

    for j in range(1, parts):
        dom_wait(2, j, gin_ref.at[dom_from(j)])
    for p in range(parts):
        back_ref[:, p * each:(p + 1) * each] = gin_ref[p]
    returned = split(back_ref[0:1, :])

    def back_tile(i, _):
        lanes = pl.ds(pl.multiple_of(i * 256, 256), 256)
        dn_ref[0:1, lanes] = slot_ref[0:1, lanes] + total(dot(returned, pick_ref[lanes, :], NT))
        return 0

    lax.fori_loop(0, nodes // 256, back_tile, 0)

    for j in range(slices):
        index = feat_from(j)
        if j % 2:
            feat_wait(3, j, mask_ref.at[index])
        for t in range(block // 128):
            lanes = pl.ds(pl.multiple_of(index * block + t * 128, 128), 128)
            grad = dl_ref[:, lanes] * col_ref[1] + dn_ref[0:1, lanes] * col_ref[2]
            keep = mask_ref[index, :, t * 128:(t + 1) * 128].astype(F32)
            dpre_ref[j, :, t * 128:(t + 1) * 128] = jnp.where(keep > 0, grad, 0.0).astype(BF)
        own = dot(feat_ref[:, span(index)], dpre_ref[j], NT)
        acc_ref[0] = acc_ref[0] + own if j else own

    half = hid // 2
    share = 2 * cols // parts
    spots = [(slice(p // 2 * share, (p // 2 + 1) * share), slice(p % 2 * half, (p % 2 + 1) * half)) for p in range(parts)]

    def send_shares(h):
        for p in range(parts):
            rs_out[h, p] = acc_ref[h, spots[p][0], spots[p][1]].astype(BF)
        for j in range(1, parts):
            dom_copy(3 + h, j, rs_out.at[h, dom_peer(j)], rs_in.at[h, d])

    if reduce_here:
        send_shares(0)
    for j in range(slices):
        other = dot(agg_ref[:, span(feat_from(j))], dpre_ref[j], NT)
        acc_ref[1] = acc_ref[1] + other if j else other
    if reduce_here:
        send_shares(1)
        side = lax.rem(d, 2)
        beside = d + 1 - 2 * side

        def hand_over(h, j, index):
            copy = pltpu.make_async_remote_copy(
                src_ref=ag_ref.at[h, index], dst_ref=ag_ref.at[h, index],
                send_sem=dom_send.at[5 + h, j], recv_sem=dom_recv.at[5 + h, j],
                device_id={"dom": beside}, device_id_type=MESH)
            copy.start()
            sent.append(copy)

        for h in range(2):
            whole = rs_out[h, d].astype(F32)
            for j in range(1, parts):
                dom_wait(3 + h, j, rs_in.at[h, dom_from(j)])
                whole = whole + rs_in[h, dom_from(j)].astype(F32)
            ag_ref[h, d] = whole.astype(BF)
            for j in range(2, parts, 2):
                dom_copy(5 + h, j, ag_ref.at[h, d], ag_ref.at[h, d])
            hand_over(h, 1, d)
        for h in range(2):
            for j in range(2, parts, 2):
                dom_wait(5 + h, j, ag_ref.at[h, dom_from(j)])
                hand_over(h, j + 1, dom_from(j))
        for h, ref in enumerate((gself_ref, gneigh_ref)):
            for j in range(1, parts, 2):
                dom_wait(5 + h, j, ag_ref.at[h, lax.rem(beside + parts + 1 - j, parts)])
            for p in range(parts):
                ref[spots[p][0], spots[p][1]] = ag_ref[h, p].astype(F32)
    else:
        gself_ref[...] = acc_ref[0]
        gneigh_ref[...] = acc_ref[1]
    for copy in sent:
        copy.wait_send()


def body(features, neighbors, degree, send_rows, labels, w_self, w_neigh, bias, a_self, a_neigh):
    parts = lax.axis_size("dom")
    slices = lax.axis_size("feat")
    cols, nodes = features.shape
    fan = neighbors.shape[0]
    each = send_rows.shape[2]
    remote = parts * each
    table = nodes + remote
    block = nodes // slices
    hid = w_self.shape[1]
    share = 2 * cols // parts
    reduce_here = parts % 2 == 0 and share * parts == 2 * cols and share % 16 == 0 and hid % 256 == 0
    scale = float(nodes * parts) ** (-0.5)
    spare = share if reduce_here else 16
    V = pltpu.VMEM
    held = [
        V((cols, nodes), BF), V((fan, nodes), jnp.int32), V((1, nodes), jnp.int32), V((parts, each), jnp.int32),
        V((1, nodes), jnp.int32), V(w_self.shape, BF), V(w_neigh.shape, BF),
        V((1, hid), F32), V((1, hid), F32), V((1, hid), F32),
    ]
    scratch = held + [
        V((fan, nodes), jnp.int32), V((fan, nodes), jnp.int32),
        V((table, nodes), BF), V((nodes, remote), BF),
        V((slices, cols, block), BF), V((slices, cols, block), BF), V((cols, nodes), BF),
        V((parts, cols, each), BF), V((parts, cols, each), BF), V((cols, remote), BF),
        V((3, hid, 128), F32), V((hid, block), F32), V((slices, hid, block), BF),
        V((slices, 8, block), F32), V((8, nodes), F32),
        V((parts, 8, each), F32), V((parts, 8, each), F32), V((8, remote), F32),
        V((16, nodes), BF), V((8, table), F32),
        V((parts, 8, each), F32), V((parts, 8, each), F32), V((8, remote), F32),
        V((8, nodes), F32), V((1, nodes), F32),
        V((2, cols, hid), F32), V((slices, hid, block), BF),
        V((2, parts, spare, hid // 2), BF), V((2, parts, spare, hid // 2), BF), V((2, parts, spare, hid // 2), BF),
        pltpu.SemaphoreType.DMA((4, slices)), pltpu.SemaphoreType.DMA((4, slices)),
        pltpu.SemaphoreType.DMA((7, parts)), pltpu.SemaphoreType.DMA((7, parts)),
        pltpu.SemaphoreType.DMA((10,)),
    ]
    vm = pl.BlockSpec(memory_space=pltpu.VMEM)
    logits, grad_self, grad_neigh = pl.pallas_call(
        functools.partial(kernel, parts, slices, reduce_here, scale),
        out_shape=(
            jax.ShapeDtypeStruct((1, nodes), F32),
            jax.ShapeDtypeStruct((cols, hid), F32),
            jax.ShapeDtypeStruct((cols, hid), F32),
        ),
        in_specs=[pl.BlockSpec(memory_space=pltpu.HBM)] * 10,
        out_specs=(vm, vm, vm),
        scratch_shapes=scratch,
        compiler_params=pltpu.CompilerParams(
            collective_id=0, has_side_effects=True, vmem_limit_bytes=62 * 1024 * 1024),
    )(
        features, neighbors, degree.reshape(1, nodes), send_rows.reshape(parts, each), labels.reshape(1, nodes),
        w_self, w_neigh, bias.reshape(1, hid), a_self.reshape(1, hid), a_neigh.reshape(1, hid),
    )
    if not reduce_here:
        grad_self, grad_neigh = lax.psum((grad_self, grad_neigh), "dom")
    return (logits.reshape(nodes), grad_self, grad_neigh)


def solution(mesh):
    return jax.shard_map(
        body,
        mesh=mesh,
        in_specs=(
            P("feat", "dom"), P(None, "dom"), P("dom"), P("dom", None, None), P("dom"),
            P(), P(), P(), P(), P(),
        ),
        out_specs=(P("dom"), P("feat", None), P("feat", None)),
        check_vma=False,
    )
```

```python
import functools

import jax
import jax.numpy as jnp
from jax import lax
from jax.experimental import pallas as pl
from jax.experimental.pallas import tpu as pltpu
from jax.sharding import PartitionSpec as P

MESH = pl.DeviceIdType.MESH
BF = jnp.bfloat16
F32 = jnp.float32
NN = (((1,), (0,)), ((), ()))
NT = (((1,), (1,)), ((), ()))
GROUPS = 6
BITS = 5


def dot(a, b, dims):
    return lax.dot_general(a, b, dims, preferred_element_type=F32)


def split(row):
    wide = jnp.broadcast_to(row, (16, row.shape[1]))
    sub = lax.broadcasted_iota(jnp.int32, wide.shape, 0)
    first = wide.astype(BF).astype(F32)
    rest = wide - first
    second = rest.astype(BF).astype(F32)
    third = rest - second
    out = jnp.where(sub == 0, first, jnp.where(sub == 1, second, jnp.where(sub == 2, third, 0.0)))
    return out.astype(BF)


def total(rows):
    return jnp.sum(rows, axis=0, keepdims=True)


def kernel(
    parts, slices, reduce_here, scale,
    *refs,
):
    inputs, refs = refs[:10], refs[10:]
    held, refs = refs[3:13], refs[:3] + refs[13:]
    run(parts, slices, reduce_here, scale, inputs, held, *refs)


def run(
    parts, slices, reduce_here, scale, inputs, held,
    logit_ref, gself_ref, gneigh_ref,
    hi_ref, val_ref, count_ref, pick_ref, fblk_ref, ablk_ref, agg_ref, out_ref, inc_ref, inctab_ref,
    col_ref, pre_ref, mask_ref, score_ref, srow_ref, sout_ref, sin_ref, stab_ref, wsplit_ref, slot_ref,
    gout_ref, gin_ref, back_ref, dn_ref, dl_ref, acc_ref, dpre_ref, rs_out, rs_in, ag_ref, wt_ref,
    feat_send, feat_recv, dom_send, dom_recv, load_sem,
):
    feat_ref, neigh_ref, degree_ref, send_ref, label_ref, ws_ref, wn_ref, bias_ref, as_ref, an_ref = held
    loads = [pltpu.make_async_copy(a, b, load_sem.at[k]) for k, (a, b) in enumerate(zip(inputs, held))]
    for k in (0, 3, 1, 2, 5, 7, 8, 9, 6, 4):
        loads[k].start()
    d = lax.axis_index("dom")
    f = lax.axis_index("feat")
    cols, nodes = feat_ref.shape
    fan = neigh_ref.shape[0]
    each = send_ref.shape[1]
    remote = parts * each
    table = nodes + remote
    block = nodes // slices
    hid = ws_ref.shape[1]
    rows = table // GROUPS
    shift = rows.bit_length() - 1

    chips = slices // 2
    chip, core = f // 2, lax.rem(f, 2)

    def feat_peer(j):
        return 2 * lax.rem(chip + j // 2, chips) + lax.rem(core + j % 2, 2)

    def feat_from(j):
        return 2 * lax.rem(chip + chips - j // 2, chips) + lax.rem(core + j % 2, 2)

    far_first = list(range(2, slices)) + [1]

    barrier = pltpu.get_barrier_semaphore()
    for j in range(1, parts):
        pl.semaphore_signal(barrier, inc=1, device_id={"dom": lax.rem(d + j, parts)}, device_id_type=MESH)
    for j in range(1, slices):
        pl.semaphore_signal(barrier, inc=1, device_id={"feat": feat_peer(j)}, device_id_type=MESH)

    sent = []

    def feat_copy(phase, j, src, dst):
        copy = pltpu.make_async_remote_copy(
            src_ref=src, dst_ref=dst, send_sem=feat_send.at[phase, j], recv_sem=feat_recv.at[phase, j],
            device_id={"feat": feat_peer(j)}, device_id_type=MESH)
        copy.start()
        sent.append(copy)

    def dom_copy(phase, j, src, dst):
        copy = pltpu.make_async_remote_copy(
            src_ref=src, dst_ref=dst, send_sem=dom_send.at[phase, j], recv_sem=dom_recv.at[phase, j],
            device_id={"dom": lax.rem(d + j, parts)}, device_id_type=MESH)
        copy.start()
        sent.append(copy)

    def forward(phase, j, src, dst):
        copy = pltpu.make_async_remote_copy(
            src_ref=src, dst_ref=dst, send_sem=feat_send.at[phase, j], recv_sem=feat_recv.at[phase, j],
            device_id={"feat": feat_peer(1)}, device_id_type=MESH)
        copy.start()
        sent.append(copy)

    def feat_wait(phase, j, dst):
        pltpu.make_async_remote_copy(
            src_ref=dst, dst_ref=dst, send_sem=feat_send.at[phase, j], recv_sem=feat_recv.at[phase, j],
            device_id={"feat": feat_peer(j)}, device_id_type=MESH).wait_recv()

    def dom_wait(phase, j, dst):
        pltpu.make_async_remote_copy(
            src_ref=dst, dst_ref=dst, send_sem=dom_send.at[phase, j], recv_sem=dom_recv.at[phase, j],
            device_id={"dom": lax.rem(d + j, parts)}, device_id_type=MESH).wait_recv()

    def dom_peer(j):
        return lax.rem(d + j, parts)

    def dom_from(j):
        return lax.rem(d + parts - j, parts)

    def span(index):
        return pl.ds(pl.multiple_of(index * block, block), block)

    loads[0].wait()
    loads[3].wait()

    def pick(i, _):
        r = pl.multiple_of(i * 256, 256)
        here = lax.broadcasted_iota(jnp.int32, (256, each), 0) + r
        for p in range(parts):
            pick_ref[pl.ds(r, 256), p * each:(p + 1) * each] = jnp.where(here == send_ref[p:p + 1, :], 1.0, 0.0).astype(BF)
        return 0

    lax.fori_loop(0, nodes // 256, pick, 0)
    step = min(256, remote)
    for c in range(remote // step):
        got = dot(feat_ref[...], pick_ref[:, c * step:(c + 1) * step], NN).astype(BF)
        for p in range(step // each):
            out_ref[c * (step // each) + p] = got[:, p * each:(p + 1) * each]
    pl.semaphore_wait(barrier, parts + slices - 2)
    for j in range(1, parts):
        dom_copy(0, j, out_ref.at[dom_peer(j)], inc_ref.at[d])
    inc_ref[d] = out_ref[d]

    for j in far_first:
        feat_copy(0, j, feat_ref.at[:, span(feat_peer(j))], fblk_ref.at[f])
    fblk_ref[f] = feat_ref[:, span(f)]

    loads[1].wait()
    loads[2].wait()
    slot = lax.broadcasted_iota(jnp.int32, (fan, nodes), 0)
    used = slot < degree_ref[...]
    hi_ref[...] = neigh_ref[...] & (rows - 1)
    val_ref[...] = jnp.where(used, jnp.left_shift(jnp.int32(1), (neigh_ref[...] >> shift) * BITS), 0)

    def count_lanes(c, first):
        lanes = pl.ds(pl.multiple_of(first + c * 128, 128), 128)
        his = [jnp.broadcast_to(hi_ref[k:k + 1, lanes], (8, 128)) for k in range(fan)]
        vals = [jnp.broadcast_to(val_ref[k:k + 1, lanes], (8, 128)) for k in range(fan)]
        base = lax.broadcasted_iota(jnp.int32, (8, 128), 0)

        def count_rows(i, _):
            for u in range(0, 32, 16):
                r = pl.multiple_of(i * 32 + u, 16)
                words = []
                for here in (base + r, base + (r + 8)):
                    terms = [jnp.where(h == here, v, 0) for h, v in zip(his, vals)]
                    while len(terms) > 1:
                        terms = [a + b for a, b in zip(terms[::2], terms[1::2])] + terms[len(terms) & ~1:]
                    words.append(terms[0])
                for g in range(GROUPS):
                    fields = [w >> (BITS * g) if g else w for w in words]
                    if g < GROUPS - 1:
                        fields = [w & ((1 << BITS) - 1) for w in fields]
                    both = jnp.concatenate([w.astype(F32) for w in fields], axis=0)
                    count_ref[pl.ds(pl.multiple_of(g * rows + r, 16), 16), lanes] = both.astype(BF)
            return 0

        lax.fori_loop(0, rows // 32, count_rows, 0)
        return first

    def count_block(index):
        lax.fori_loop(0, block // 128, count_lanes, index * block)

    for j in far_first:
        count_block(feat_peer(j))
    inverse = 1.0 / degree_ref[...].astype(F32)

    for k in (7, 8, 9):
        loads[k].wait()
    for k, ref in enumerate((bias_ref, as_ref, an_ref)):
        col_ref[k] = jnp.broadcast_to(ref[...], (128, hid)).T

    for j in range(1, parts):
        dom_wait(0, j, inc_ref.at[dom_from(j)])
    for p in range(parts):
        inctab_ref[:, p * each:(p + 1) * each] = inc_ref[p]

    tile = min(256, block)

    def aggregate(index):
        for t in range(block // tile):
            lanes = pl.ds(pl.multiple_of(index * block + t * tile, tile), tile)
            sums = dot(feat_ref[...], count_ref[:nodes, lanes], NN)
            sums = sums + dot(inctab_ref[...], count_ref[nodes:, lanes], NN)
            agg_ref[:, lanes] = (sums * (1.0 / degree_ref[:, lanes].astype(F32))).astype(BF)

    for j in far_first:
        aggregate(feat_peer(j))
        feat_copy(1, j, agg_ref.at[:, span(feat_peer(j))], ablk_ref.at[f])
    count_block(f)
    aggregate(f)
    ablk_ref[f] = agg_ref[:, span(f)]

    for j in range(1, slices):
        feat_wait(0, j, fblk_ref.at[feat_from(j)])
    depth = slices * cols
    loads[5].wait()
    loads[6].wait()
    wt_ref[0] = ws_ref[...].T
    wt_ref[1] = wn_ref[...].T
    pre_ref[...] = dot(wt_ref[0], fblk_ref[...].reshape(depth, block), NN)
    for j in range(1, slices):
        feat_wait(1, j, ablk_ref.at[feat_from(j)])
    pre_ref[...] += dot(wt_ref[1], ablk_ref[...].reshape(depth, block), NN)
    for t in range(block // 128):
        pre = pre_ref[:, t * 128:(t + 1) * 128] + col_ref[0]
        hidden = jnp.maximum(pre, 0.0)
        mask_ref[f, :, t * 128:(t + 1) * 128] = jnp.where(pre > 0, 1.0, 0.0).astype(BF)
        own = jnp.broadcast_to(total(hidden * col_ref[1]), (8, 128))
        other = jnp.broadcast_to(total(hidden * col_ref[2]), (8, 128))
        sub = lax.broadcasted_iota(jnp.int32, (8, 128), 0)
        score_ref[f, :, t * 128:(t + 1) * 128] = jnp.where(sub == 0, own, other)
    for j in far_first:
        feat_copy(2, j, score_ref.at[f], score_ref.at[f])
    for j in range(2, slices, 2):
        feat_copy(3, j, mask_ref.at[f], mask_ref.at[f])
    feat_copy(3, 1, mask_ref.at[f], mask_ref.at[f])

    for j in range(1, slices):
        feat_wait(2, j, score_ref.at[feat_from(j)])
    for s in range(slices):
        srow_ref[:, s * block:(s + 1) * block] = score_ref[s]
    own_score = split(srow_ref[1:2, :])
    boundary = total(dot(own_score, pick_ref[...], NN))
    for p in range(parts):
        sout_ref[p] = jnp.broadcast_to(boundary[:, p * each:(p + 1) * each], (8, each))
    for j in range(1, parts):
        dom_copy(1, j, sout_ref.at[dom_peer(j)], sin_ref.at[d])
    sin_ref[d] = sout_ref[d]

    def own_tile(i):
        lanes = slice(i * 256, (i + 1) * 256)
        slot_ref[0:1, lanes] = total(dot(own_score, count_ref[:nodes, lanes], NN))

    for i in range(0, nodes // 256):
        own_tile(i)
    for j in range(1, parts):
        dom_wait(1, j, sin_ref.at[dom_from(j)])
    for p in range(parts):
        stab_ref[:, p * each:(p + 1) * each] = sin_ref[p]
    spread = split(stab_ref[0:1, :])

    def logit_tile(i):
        lanes = slice(i * 256, (i + 1) * 256)
        slot_ref[0:1, lanes] += total(dot(spread, count_ref[nodes:, lanes], NN))

    for i in range(0, nodes // 256):
        logit_tile(i)
    logits = srow_ref[0:1, :] + slot_ref[0:1, :nodes] * inverse
    logit_ref[...] = logits
    loads[4].wait()
    dlogit = (1.0 / (1.0 + jnp.exp(-logits)) - label_ref[...].astype(F32)) * scale
    dl_ref[...] = dlogit
    wsplit_ref[...] = split(dlogit * inverse)

    def slot_tile(i):
        lanes = slice(i * 256, (i + 1) * 256)
        slot_ref[0:1, lanes] = total(dot(wsplit_ref[...], count_ref[lanes, :], NT))

    for i in range(nodes // 256, table // 256):
        slot_tile(i)
    for p in range(parts):
        gout_ref[p] = jnp.broadcast_to(slot_ref[0:1, nodes + p * each:nodes + (p + 1) * each], (8, each))
    for j in range(1, parts):
        dom_copy(2, j, gout_ref.at[dom_peer(j)], gin_ref.at[d])
    gin_ref[d] = gout_ref[d]
    for i in range(0, nodes // 256):
        slot_tile(i)

    for j in range(2, slices, 2):
        feat_wait(3, j, mask_ref.at[feat_from(j)])
        index = feat_from(j)
        forward(3, j + 1, mask_ref.at[index], mask_ref.at[index])

    for j in range(1, parts):
        dom_wait(2, j, gin_ref.at[dom_from(j)])
    for p in range(parts):
        back_ref[:, p * each:(p + 1) * each] = gin_ref[p]
    returned = split(back_ref[0:1, :])

    def back_tile(i):
        lanes = slice(i * 256, (i + 1) * 256)
        dn_ref[0:1, lanes] = slot_ref[0:1, lanes] + total(dot(returned, pick_ref[lanes, :], NT))

    for i in range(0, nodes // 256):
        back_tile(i)

    for j in range(slices):
        index = feat_from(j)
        if j % 2:
            feat_wait(3, j, mask_ref.at[index])
        for t in range(block // 128):
            lanes = pl.ds(pl.multiple_of(index * block + t * 128, 128), 128)
            grad = dl_ref[:, lanes] * col_ref[1] + dn_ref[0:1, lanes] * col_ref[2]
            dpre_ref[j, :, t * 128:(t + 1) * 128] = grad.astype(BF) * mask_ref[index, :, t * 128:(t + 1) * 128]
        own = dot(feat_ref[:, span(index)], dpre_ref[j], NT)
        acc_ref[0] = acc_ref[0] + own if j else own

    half = hid // 2
    share = 2 * cols // parts
    spots = [(slice(p // 2 * share, (p // 2 + 1) * share), slice(p % 2 * half, (p % 2 + 1) * half)) for p in range(parts)]

    def send_shares(h):
        for p in range(parts):
            rs_out[h, p] = acc_ref[h, spots[p][0], spots[p][1]].astype(BF)
        for j in range(1, parts):
            dom_copy(3 + h, j, rs_out.at[h, dom_peer(j)], rs_in.at[h, d])

    if reduce_here:
        send_shares(0)
    for j in range(slices):
        other = dot(agg_ref[:, span(feat_from(j))], dpre_ref[j], NT)
        acc_ref[1] = acc_ref[1] + other if j else other
    if reduce_here:
        send_shares(1)
        side = lax.rem(d, 2)
        beside = d + 1 - 2 * side

        def hand_over(h, j, index):
            copy = pltpu.make_async_remote_copy(
                src_ref=ag_ref.at[h, index], dst_ref=ag_ref.at[h, index],
                send_sem=dom_send.at[5 + h, j], recv_sem=dom_recv.at[5 + h, j],
                device_id={"dom": beside}, device_id_type=MESH)
            copy.start()
            sent.append(copy)

        for h in range(2):
            whole = rs_out[h, d].astype(F32)
            for j in range(1, parts):
                dom_wait(3 + h, j, rs_in.at[h, dom_from(j)])
                whole = whole + rs_in[h, dom_from(j)].astype(F32)
            ag_ref[h, d] = whole.astype(BF)
            for j in range(2, parts, 2):
                dom_copy(5 + h, j, ag_ref.at[h, d], ag_ref.at[h, d])
            hand_over(h, 1, d)
        for h in range(2):
            for j in range(2, parts, 2):
                dom_wait(5 + h, j, ag_ref.at[h, dom_from(j)])
                hand_over(h, j + 1, dom_from(j))
        for h, ref in enumerate((gself_ref, gneigh_ref)):
            for j in range(1, parts, 2):
                dom_wait(5 + h, j, ag_ref.at[h, lax.rem(beside + parts + 1 - j, parts)])
            for p in range(parts):
                ref[spots[p][0], spots[p][1]] = ag_ref[h, p].astype(F32)
    else:
        gself_ref[...] = acc_ref[0]
        gneigh_ref[...] = acc_ref[1]
    for copy in sent:
        copy.wait_send()


def place(*refs):
    sems = refs[6]
    copies = [pltpu.make_async_copy(refs[k], refs[3 + k], sems.at[k]) for k in range(3)]
    for copy in copies:
        copy.start()
    for copy in copies:
        copy.wait()


def body(features, neighbors, degree, send_rows, labels, w_self, w_neigh, bias, a_self, a_neigh):
    parts = lax.axis_size("dom")
    slices = lax.axis_size("feat")
    cols, nodes = features.shape
    fan = neighbors.shape[0]
    each = send_rows.shape[2]
    remote = parts * each
    table = nodes + remote
    block = nodes // slices
    hid = w_self.shape[1]
    share = 2 * cols // parts
    reduce_here = parts % 2 == 0 and share * parts == 2 * cols and share % 16 == 0 and hid % 256 == 0
    scale = float(nodes * parts) ** (-0.5)
    spare = share if reduce_here else 16
    V = pltpu.VMEM
    held = [
        V((cols, nodes), BF), V((fan, nodes), jnp.int32), V((1, nodes), jnp.int32), V((parts, each), jnp.int32),
        V((1, nodes), jnp.int32), V(w_self.shape, BF), V(w_neigh.shape, BF),
        V((1, hid), F32), V((1, hid), F32), V((1, hid), F32),
    ]
    scratch = held + [
        V((fan, nodes), jnp.int32), V((fan, nodes), jnp.int32),
        V((table, nodes), BF), V((nodes, remote), BF),
        V((slices, cols, block), BF), V((slices, cols, block), BF), V((cols, nodes), BF),
        V((parts, cols, each), BF), V((parts, cols, each), BF), V((cols, remote), BF),
        V((3, hid, 128), F32), V((hid, block), F32), V((slices, hid, block), BF),
        V((slices, 8, block), F32), V((8, nodes), F32),
        V((parts, 8, each), F32), V((parts, 8, each), F32), V((8, remote), F32),
        V((16, nodes), BF), V((8, table), F32),
        V((parts, 8, each), F32), V((parts, 8, each), F32), V((8, remote), F32),
        V((8, nodes), F32), V((1, nodes), F32),
        V((2, cols, hid), F32), V((slices, hid, block), BF),
        V((2, parts, spare, hid // 2), BF), V((2, parts, spare, hid // 2), BF), V((2, parts, spare, hid // 2), BF),
        V((2, hid, w_self.shape[0]), BF),
        pltpu.SemaphoreType.DMA((4, slices)), pltpu.SemaphoreType.DMA((4, slices)),
        pltpu.SemaphoreType.DMA((7, parts)), pltpu.SemaphoreType.DMA((7, parts)),
        pltpu.SemaphoreType.DMA((10,)),
    ]
    vm = pl.BlockSpec(memory_space=pltpu.VMEM)
    logits, grad_self, grad_neigh = pl.pallas_call(
        functools.partial(kernel, parts, slices, reduce_here, scale),
        out_shape=(
            jax.ShapeDtypeStruct((1, nodes), F32),
            jax.ShapeDtypeStruct((cols, hid), F32),
            jax.ShapeDtypeStruct((cols, hid), F32),
        ),
        in_specs=[pl.BlockSpec(memory_space=pltpu.HBM)] * 10,
        out_specs=(vm, vm, vm),
        scratch_shapes=scratch,
        compiler_params=pltpu.CompilerParams(
            collective_id=0, has_side_effects=True, vmem_limit_bytes=62 * 1024 * 1024),
    )(
        features, neighbors, degree.reshape(1, nodes), send_rows.reshape(parts, each), labels.reshape(1, nodes),
        w_self, w_neigh, bias.reshape(1, hid), a_self.reshape(1, hid), a_neigh.reshape(1, hid),
    )
    if reduce_here:
        hbm = pl.BlockSpec(memory_space=pltpu.HBM)
        logits, grad_self, grad_neigh = pl.pallas_call(
            place,
            out_shape=tuple(jax.ShapeDtypeStruct(x.shape, x.dtype) for x in (logits, grad_self, grad_neigh)),
            in_specs=[hbm] * 3,
            out_specs=(hbm, hbm, hbm),
            scratch_shapes=[pltpu.SemaphoreType.DMA((3,))],
            compiler_params=pltpu.CompilerParams(vmem_limit_bytes=62 * 1024 * 1024),
        )(logits, grad_self, grad_neigh)
    else:
        grad_self, grad_neigh = lax.psum((grad_self, grad_neigh), "dom")
    return (logits.reshape(nodes), grad_self, grad_neigh)


def solution(mesh):
    return jax.shard_map(
        body,
        mesh=mesh,
        in_specs=(
            P("feat", "dom"), P(None, "dom"), P("dom"), P("dom", None, None), P("dom"),
            P(), P(), P(), P(), P(),
        ),
        out_specs=(P("dom"), P("feat", None), P("feat", None)),
        check_vma=False,
    )
```

```python
import functools

import jax
import jax.numpy as jnp
from jax import lax
from jax.experimental import pallas as pl
from jax.experimental.pallas import tpu as pltpu
from jax.sharding import PartitionSpec as P

MESH = pl.DeviceIdType.MESH
BF = jnp.bfloat16
F32 = jnp.float32
NN = (((1,), (0,)), ((), ()))
NT = (((1,), (1,)), ((), ()))
GROUPS = 6
BITS = 5


def dot(a, b, dims):
    return lax.dot_general(a, b, dims, preferred_element_type=F32)


def split(row):
    wide = jnp.broadcast_to(row, (16, row.shape[1]))
    sub = lax.broadcasted_iota(jnp.int32, wide.shape, 0)
    first = wide.astype(BF).astype(F32)
    rest = wide - first
    second = rest.astype(BF).astype(F32)
    third = rest - second
    out = jnp.where(sub == 0, first, jnp.where(sub == 1, second, jnp.where(sub == 2, third, 0.0)))
    return out.astype(BF)


def total(rows):
    return jnp.sum(rows, axis=0, keepdims=True)


def kernel(
    parts, slices, reduce_here, scale,
    *refs,
):
    inputs, refs = refs[:10], refs[10:]
    held, refs = refs[3:13], refs[:3] + refs[13:]
    run(parts, slices, reduce_here, scale, inputs, held, *refs)


def run(
    parts, slices, reduce_here, scale, inputs, held,
    logit_ref, gself_ref, gneigh_ref,
    hi_ref, val_ref, count_ref, pick_ref, fblk_ref, ablk_ref, agg_ref, out_ref, inc_ref, inctab_ref,
    col_ref, pre_ref, mask_ref, score_ref, srow_ref, sout_ref, sin_ref, stab_ref, wsplit_ref, slot_ref,
    gout_ref, gin_ref, back_ref, dn_ref, dl_ref, acc_ref, dpre_ref, rs_out, rs_in, ag_ref, wt_ref,
    feat_send, feat_recv, dom_send, dom_recv, load_sem,
):
    feat_ref, neigh_ref, degree_ref, send_ref, label_ref, ws_ref, wn_ref, bias_ref, as_ref, an_ref = held
    loads = [pltpu.make_async_copy(a, b, load_sem.at[k]) for k, (a, b) in enumerate(zip(inputs, held))]
    for k in (0, 3, 1, 2, 5, 7, 8, 9, 6, 4):
        loads[k].start()
    d = lax.axis_index("dom")
    f = lax.axis_index("feat")
    cols, nodes = feat_ref.shape
    fan = neigh_ref.shape[0]
    each = send_ref.shape[1]
    remote = parts * each
    table = nodes + remote
    block = nodes // slices
    hid = ws_ref.shape[1]
    rows = table // GROUPS
    shift = rows.bit_length() - 1

    chips = slices // 2
    chip, core = f // 2, lax.rem(f, 2)

    def feat_peer(j):
        return 2 * lax.rem(chip + j // 2, chips) + lax.rem(core + j % 2, 2)

    def feat_from(j):
        return 2 * lax.rem(chip + chips - j // 2, chips) + lax.rem(core + j % 2, 2)

    far_first = list(range(2, slices)) + [1]

    barrier = pltpu.get_barrier_semaphore()
    for j in range(1, parts):
        pl.semaphore_signal(barrier, inc=1, device_id={"dom": lax.rem(d + j, parts)}, device_id_type=MESH)
    for j in range(1, slices):
        pl.semaphore_signal(barrier, inc=1, device_id={"feat": feat_peer(j)}, device_id_type=MESH)

    sent = []

    def feat_copy(phase, j, src, dst):
        copy = pltpu.make_async_remote_copy(
            src_ref=src, dst_ref=dst, send_sem=feat_send.at[phase, j], recv_sem=feat_recv.at[phase, j],
            device_id={"feat": feat_peer(j)}, device_id_type=MESH)
        copy.start()
        sent.append(copy)

    def dom_copy(phase, j, src, dst):
        copy = pltpu.make_async_remote_copy(
            src_ref=src, dst_ref=dst, send_sem=dom_send.at[phase, j], recv_sem=dom_recv.at[phase, j],
            device_id={"dom": lax.rem(d + j, parts)}, device_id_type=MESH)
        copy.start()
        sent.append(copy)

    def forward(phase, j, src, dst):
        copy = pltpu.make_async_remote_copy(
            src_ref=src, dst_ref=dst, send_sem=feat_send.at[phase, j], recv_sem=feat_recv.at[phase, j],
            device_id={"feat": feat_peer(1)}, device_id_type=MESH)
        copy.start()
        sent.append(copy)

    def feat_wait(phase, j, dst):
        pltpu.make_async_remote_copy(
            src_ref=dst, dst_ref=dst, send_sem=feat_send.at[phase, j], recv_sem=feat_recv.at[phase, j],
            device_id={"feat": feat_peer(j)}, device_id_type=MESH).wait_recv()

    def dom_wait(phase, j, dst):
        pltpu.make_async_remote_copy(
            src_ref=dst, dst_ref=dst, send_sem=dom_send.at[phase, j], recv_sem=dom_recv.at[phase, j],
            device_id={"dom": lax.rem(d + j, parts)}, device_id_type=MESH).wait_recv()

    def dom_peer(j):
        return lax.rem(d + j, parts)

    def dom_from(j):
        return lax.rem(d + parts - j, parts)

    def span(index):
        return pl.ds(pl.multiple_of(index * block, block), block)

    loads[0].wait()
    loads[3].wait()

    def pick(i, _):
        r = pl.multiple_of(i * 256, 256)
        here = lax.broadcasted_iota(jnp.int32, (256, each), 0) + r
        for p in range(parts):
            pick_ref[pl.ds(r, 256), p * each:(p + 1) * each] = jnp.where(here == send_ref[p:p + 1, :], 1.0, 0.0).astype(BF)
        return 0

    lax.fori_loop(0, nodes // 256, pick, 0)
    step = min(256, remote)
    for c in range(remote // step):
        got = dot(feat_ref[...], pick_ref[:, c * step:(c + 1) * step], NN).astype(BF)
        for p in range(step // each):
            out_ref[c * (step // each) + p] = got[:, p * each:(p + 1) * each]
    pl.semaphore_wait(barrier, parts + slices - 2)
    cuts = 2 if cols % 32 == 0 else 1
    bands = [slice(c * cols // cuts, (c + 1) * cols // cuts) for c in range(cuts)]
    for c, band in enumerate(bands):
        for j in range(1, parts):
            dom_copy(7 * c, j, out_ref.at[dom_peer(j), band], inc_ref.at[d, band])
    inc_ref[d] = out_ref[d]

    for j in far_first:
        feat_copy(0, j, feat_ref.at[:, span(feat_peer(j))], fblk_ref.at[f])
    fblk_ref[f] = feat_ref[:, span(f)]

    loads[1].wait()
    loads[2].wait()
    slot = lax.broadcasted_iota(jnp.int32, (fan, nodes), 0)
    used = slot < degree_ref[...]
    hi_ref[...] = neigh_ref[...] & (rows - 1)
    val_ref[...] = jnp.where(used, jnp.left_shift(jnp.int32(1), (neigh_ref[...] >> shift) * BITS), 0)

    def count_lanes(c, first):
        lanes = pl.ds(pl.multiple_of(first + c * 128, 128), 128)
        his = [jnp.broadcast_to(hi_ref[k:k + 1, lanes], (8, 128)) for k in range(fan)]
        vals = [jnp.broadcast_to(val_ref[k:k + 1, lanes], (8, 128)) for k in range(fan)]
        base = lax.broadcasted_iota(jnp.int32, (8, 128), 0)

        def count_rows(i, _):
            for u in range(0, 32, 16):
                r = pl.multiple_of(i * 32 + u, 16)
                words = []
                for here in (base + r, base + (r + 8)):
                    terms = [jnp.where(h == here, v, 0) for h, v in zip(his, vals)]
                    while len(terms) > 1:
                        terms = [a + b for a, b in zip(terms[::2], terms[1::2])] + terms[len(terms) & ~1:]
                    words.append(terms[0])
                for g in range(GROUPS):
                    fields = [w >> (BITS * g) if g else w for w in words]
                    if g < GROUPS - 1:
                        fields = [w & ((1 << BITS) - 1) for w in fields]
                    both = jnp.concatenate([w.astype(F32) for w in fields], axis=0)
                    count_ref[pl.ds(pl.multiple_of(g * rows + r, 16), 16), lanes] = both.astype(BF)
            return 0

        lax.fori_loop(0, rows // 32, count_rows, 0)
        return first

    def count_block(index):
        lax.fori_loop(0, block // 128, count_lanes, index * block)

    far = far_first[:-1]
    for j in far:
        count_block(feat_peer(j))
    inverse = 1.0 / degree_ref[...].astype(F32)

    for k in (7, 8, 9):
        loads[k].wait()
    for k, ref in enumerate((bias_ref, as_ref, an_ref)):
        col_ref[k] = jnp.broadcast_to(ref[...], (128, hid)).T

    tile = min(256, block)

    def aggregate(index, band):
        for t in range(block // tile):
            lanes = pl.ds(pl.multiple_of(index * block + t * tile, tile), tile)
            sums = dot(feat_ref[band, :], count_ref[:nodes, lanes], NN)
            sums = sums + dot(inctab_ref[band, :], count_ref[nodes:, lanes], NN)
            agg_ref[band, lanes] = (sums * (1.0 / degree_ref[:, lanes].astype(F32))).astype(BF)

    for c, band in enumerate(bands):
        if c == cuts - 1:
            count_block(feat_peer(1))
        for j in range(1, parts):
            dom_wait(7 * c, j, inc_ref.at[dom_from(j), band])
        for p in range(parts):
            inctab_ref[band, p * each:(p + 1) * each] = inc_ref[p, band]
        for j in far:
            aggregate(feat_peer(j), band)
            feat_copy(1 + 3 * c, j, agg_ref.at[band, span(feat_peer(j))], ablk_ref.at[f, band])
    whole_band = slice(0, cols)
    aggregate(feat_peer(1), whole_band)
    feat_copy(1, 1, agg_ref.at[:, span(feat_peer(1))], ablk_ref.at[f])
    count_block(f)
    aggregate(f, whole_band)
    ablk_ref[f] = agg_ref[:, span(f)]

    for j in range(1, slices):
        feat_wait(0, j, fblk_ref.at[feat_from(j)])
    depth = slices * cols
    loads[5].wait()
    loads[6].wait()
    wt_ref[0] = ws_ref[...].T
    wt_ref[1] = wn_ref[...].T
    pre_ref[...] = dot(wt_ref[0], fblk_ref[...].reshape(depth, block), NN)
    feat_wait(1, 1, ablk_ref.at[feat_from(1)])
    for c, band in enumerate(bands):
        for j in far:
            feat_wait(1 + 3 * c, j, ablk_ref.at[feat_from(j), band])
    pre_ref[...] += dot(wt_ref[1], ablk_ref[...].reshape(depth, block), NN)
    for t in range(block // 128):
        pre = pre_ref[:, t * 128:(t + 1) * 128] + col_ref[0]
        hidden = jnp.maximum(pre, 0.0)
        mask_ref[f, :, t * 128:(t + 1) * 128] = jnp.where(pre > 0, 1.0, 0.0).astype(BF)
        own = jnp.broadcast_to(total(hidden * col_ref[1]), (8, 128))
        other = jnp.broadcast_to(total(hidden * col_ref[2]), (8, 128))
        sub = lax.broadcasted_iota(jnp.int32, (8, 128), 0)
        score_ref[f, :, t * 128:(t + 1) * 128] = jnp.where(sub == 0, own, other)
    for j in far_first:
        feat_copy(2, j, score_ref.at[f], score_ref.at[f])
    for j in range(2, slices, 2):
        feat_copy(3, j, mask_ref.at[f], mask_ref.at[f])
    feat_copy(3, 1, mask_ref.at[f], mask_ref.at[f])

    for j in range(1, slices):
        feat_wait(2, j, score_ref.at[feat_from(j)])
    for s in range(slices):
        srow_ref[:, s * block:(s + 1) * block] = score_ref[s]
    own_score = split(srow_ref[1:2, :])
    boundary = total(dot(own_score, pick_ref[...], NN))
    for p in range(parts):
        sout_ref[p] = jnp.broadcast_to(boundary[:, p * each:(p + 1) * each], (8, each))
    for j in range(1, parts):
        dom_copy(1, j, sout_ref.at[dom_peer(j)], sin_ref.at[d])
    sin_ref[d] = sout_ref[d]

    def own_tile(i):
        lanes = slice(i * 256, (i + 1) * 256)
        slot_ref[0:1, lanes] = total(dot(own_score, count_ref[:nodes, lanes], NN))

    for i in range(0, nodes // 256):
        own_tile(i)
    for j in range(1, parts):
        dom_wait(1, j, sin_ref.at[dom_from(j)])
    for p in range(parts):
        stab_ref[:, p * each:(p + 1) * each] = sin_ref[p]
    spread = split(stab_ref[0:1, :])

    def logit_tile(i):
        lanes = slice(i * 256, (i + 1) * 256)
        slot_ref[0:1, lanes] += total(dot(spread, count_ref[nodes:, lanes], NN))

    for i in range(0, nodes // 256):
        logit_tile(i)
    logits = srow_ref[0:1, :] + slot_ref[0:1, :nodes] * inverse
    logit_ref[...] = logits
    loads[4].wait()
    dlogit = (1.0 / (1.0 + jnp.exp(-logits)) - label_ref[...].astype(F32)) * scale
    dl_ref[...] = dlogit
    wsplit_ref[...] = split(dlogit * inverse)

    def slot_tile(i):
        lanes = slice(i * 256, (i + 1) * 256)
        slot_ref[0:1, lanes] = total(dot(wsplit_ref[...], count_ref[lanes, :], NT))

    for i in range(nodes // 256, table // 256):
        slot_tile(i)
    for p in range(parts):
        gout_ref[p] = jnp.broadcast_to(slot_ref[0:1, nodes + p * each:nodes + (p + 1) * each], (8, each))
    for j in range(1, parts):
        dom_copy(2, j, gout_ref.at[dom_peer(j)], gin_ref.at[d])
    gin_ref[d] = gout_ref[d]
    for i in range(0, nodes // 256):
        slot_tile(i)

    for j in range(2, slices, 2):
        feat_wait(3, j, mask_ref.at[feat_from(j)])
        index = feat_from(j)
        forward(3, j + 1, mask_ref.at[index], mask_ref.at[index])

    for j in range(1, parts):
        dom_wait(2, j, gin_ref.at[dom_from(j)])
    for p in range(parts):
        back_ref[:, p * each:(p + 1) * each] = gin_ref[p]
    returned = split(back_ref[0:1, :])

    def back_tile(i):
        lanes = slice(i * 256, (i + 1) * 256)
        dn_ref[0:1, lanes] = slot_ref[0:1, lanes] + total(dot(returned, pick_ref[lanes, :], NT))

    for i in range(0, nodes // 256):
        back_tile(i)

    for j in range(slices):
        index = feat_from(j)
        if j % 2:
            feat_wait(3, j, mask_ref.at[index])
        for t in range(block // 128):
            lanes = pl.ds(pl.multiple_of(index * block + t * 128, 128), 128)
            grad = dl_ref[:, lanes] * col_ref[1] + dn_ref[0:1, lanes] * col_ref[2]
            dpre_ref[j, :, t * 128:(t + 1) * 128] = grad.astype(BF) * mask_ref[index, :, t * 128:(t + 1) * 128]
        own = dot(feat_ref[:, span(index)], dpre_ref[j], NT)
        acc_ref[0] = acc_ref[0] + own if j else own

    half = hid // 2
    share = 2 * cols // parts
    spots = [(slice(p // 2 * share, (p // 2 + 1) * share), slice(p % 2 * half, (p % 2 + 1) * half)) for p in range(parts)]

    def send_shares(h):
        for p in range(parts):
            rs_out[h, p] = acc_ref[h, spots[p][0], spots[p][1]].astype(BF)
        for j in range(1, parts):
            dom_copy(3 + h, j, rs_out.at[h, dom_peer(j)], rs_in.at[h, d])

    if reduce_here:
        send_shares(0)
    for j in range(slices):
        other = dot(agg_ref[:, span(feat_from(j))], dpre_ref[j], NT)
        acc_ref[1] = acc_ref[1] + other if j else other
    if reduce_here:
        send_shares(1)
        side = lax.rem(d, 2)
        beside = d + 1 - 2 * side

        def hand_over(h, j, index):
            copy = pltpu.make_async_remote_copy(
                src_ref=ag_ref.at[h, index], dst_ref=ag_ref.at[h, index],
                send_sem=dom_send.at[5 + h, j], recv_sem=dom_recv.at[5 + h, j],
                device_id={"dom": beside}, device_id_type=MESH)
            copy.start()
            sent.append(copy)

        for h in range(2):
            whole = rs_out[h, d].astype(F32)
            for j in range(1, parts):
                dom_wait(3 + h, j, rs_in.at[h, dom_from(j)])
                whole = whole + rs_in[h, dom_from(j)].astype(F32)
            ag_ref[h, d] = whole.astype(BF)
            for j in range(2, parts, 2):
                dom_copy(5 + h, j, ag_ref.at[h, d], ag_ref.at[h, d])
            hand_over(h, 1, d)
        for h in range(2):
            for j in range(2, parts, 2):
                dom_wait(5 + h, j, ag_ref.at[h, dom_from(j)])
                hand_over(h, j + 1, dom_from(j))
        for h, ref in enumerate((gself_ref, gneigh_ref)):
            for j in range(1, parts, 2):
                dom_wait(5 + h, j, ag_ref.at[h, lax.rem(beside + parts + 1 - j, parts)])
            for p in range(parts):
                ref[spots[p][0], spots[p][1]] = ag_ref[h, p]
    else:
        gself_ref[...] = acc_ref[0]
        gneigh_ref[...] = acc_ref[1]
    for copy in sent:
        copy.wait_send()


def place(logit_ref, gself_ref, gneigh_ref, logit_out, gself_out, gneigh_out):
    logit_out[...] = logit_ref[...]
    gself_out[...] = gself_ref[...].astype(F32)
    gneigh_out[...] = gneigh_ref[...].astype(F32)


def body(features, neighbors, degree, send_rows, labels, w_self, w_neigh, bias, a_self, a_neigh):
    parts = lax.axis_size("dom")
    slices = lax.axis_size("feat")
    cols, nodes = features.shape
    fan = neighbors.shape[0]
    each = send_rows.shape[2]
    remote = parts * each
    table = nodes + remote
    block = nodes // slices
    hid = w_self.shape[1]
    share = 2 * cols // parts
    reduce_here = parts % 2 == 0 and share * parts == 2 * cols and share % 16 == 0 and hid % 256 == 0
    scale = float(nodes * parts) ** (-0.5)
    spare = share if reduce_here else 16
    V = pltpu.VMEM
    held = [
        V((cols, nodes), BF), V((fan, nodes), jnp.int32), V((1, nodes), jnp.int32), V((parts, each), jnp.int32),
        V((1, nodes), jnp.int32), V(w_self.shape, BF), V(w_neigh.shape, BF),
        V((1, hid), F32), V((1, hid), F32), V((1, hid), F32),
    ]
    scratch = held + [
        V((fan, nodes), jnp.int32), V((fan, nodes), jnp.int32),
        V((table, nodes), BF), V((nodes, remote), BF),
        V((slices, cols, block), BF), V((slices, cols, block), BF), V((cols, nodes), BF),
        V((parts, cols, each), BF), V((parts, cols, each), BF), V((cols, remote), BF),
        V((3, hid, 128), F32), V((hid, block), F32), V((slices, hid, block), BF),
        V((slices, 8, block), F32), V((8, nodes), F32),
        V((parts, 8, each), F32), V((parts, 8, each), F32), V((8, remote), F32),
        V((16, nodes), BF), V((8, table), F32),
        V((parts, 8, each), F32), V((parts, 8, each), F32), V((8, remote), F32),
        V((8, nodes), F32), V((1, nodes), F32),
        V((2, cols, hid), F32), V((slices, hid, block), BF),
        V((2, parts, spare, hid // 2), BF), V((2, parts, spare, hid // 2), BF), V((2, parts, spare, hid // 2), BF),
        V((2, hid, w_self.shape[0]), BF),
        pltpu.SemaphoreType.DMA((5, slices)), pltpu.SemaphoreType.DMA((5, slices)),
        pltpu.SemaphoreType.DMA((8, parts)), pltpu.SemaphoreType.DMA((8, parts)),
        pltpu.SemaphoreType.DMA((10,)),
    ]
    vm = pl.BlockSpec(memory_space=pltpu.VMEM)
    logits, grad_self, grad_neigh = pl.pallas_call(
        functools.partial(kernel, parts, slices, reduce_here, scale),
        out_shape=(
            jax.ShapeDtypeStruct((1, nodes), F32),
            jax.ShapeDtypeStruct((cols, hid), BF if reduce_here else F32),
            jax.ShapeDtypeStruct((cols, hid), BF if reduce_here else F32),
        ),
        in_specs=[pl.BlockSpec(memory_space=pltpu.HBM)] * 10,
        out_specs=(vm, vm, vm),
        scratch_shapes=scratch,
        compiler_params=pltpu.CompilerParams(
            collective_id=0, has_side_effects=True, vmem_limit_bytes=62 * 1024 * 1024),
    )(
        features, neighbors, degree.reshape(1, nodes), send_rows.reshape(parts, each), labels.reshape(1, nodes),
        w_self, w_neigh, bias.reshape(1, hid), a_self.reshape(1, hid), a_neigh.reshape(1, hid),
    )
    if reduce_here:
        logits, grad_self, grad_neigh = pl.pallas_call(
            place,
            out_shape=tuple(jax.ShapeDtypeStruct(x.shape, F32) for x in (logits, grad_self, grad_neigh)),
            in_specs=[vm] * 3,
            out_specs=(vm, vm, vm),
            compiler_params=pltpu.CompilerParams(vmem_limit_bytes=62 * 1024 * 1024),
        )(logits, grad_self, grad_neigh)
    else:
        grad_self, grad_neigh = lax.psum((grad_self, grad_neigh), "dom")
    return (logits.reshape(nodes), grad_self, grad_neigh)


def solution(mesh):
    return jax.shard_map(
        body,
        mesh=mesh,
        in_specs=(
            P("feat", "dom"), P(None, "dom"), P("dom"), P("dom", None, None), P("dom"),
            P(), P(), P(), P(), P(),
        ),
        out_specs=(P("dom"), P("feat", None), P("feat", None)),
        check_vma=False,
    )
```

```python
import functools

import jax
import jax.numpy as jnp
from jax import lax
from jax.experimental import pallas as pl
from jax.experimental.pallas import tpu as pltpu
from jax.sharding import PartitionSpec as P

MESH = pl.DeviceIdType.MESH
BF = jnp.bfloat16
F32 = jnp.float32
NN = (((1,), (0,)), ((), ()))
NT = (((1,), (1,)), ((), ()))
GROUPS = 6
BITS = 5


def dot(a, b, dims):
    return lax.dot_general(a, b, dims, preferred_element_type=F32)


def split(row):
    wide = jnp.broadcast_to(row, (16, row.shape[1]))
    sub = lax.broadcasted_iota(jnp.int32, wide.shape, 0)
    first = wide.astype(BF).astype(F32)
    rest = wide - first
    second = rest.astype(BF).astype(F32)
    third = rest - second
    out = jnp.where(sub == 0, first, jnp.where(sub == 1, second, jnp.where(sub == 2, third, 0.0)))
    return out.astype(BF)


def total(rows):
    return jnp.sum(rows, axis=0, keepdims=True)


def kernel(
    parts, slices, reduce_here, scale,
    *refs,
):
    inputs, refs = refs[:10], refs[10:]
    held, refs = refs[3:13], refs[:3] + refs[13:]
    run(parts, slices, reduce_here, scale, inputs, held, *refs)


def run(
    parts, slices, reduce_here, scale, inputs, held,
    logit_ref, gself_ref, gneigh_ref,
    hi_ref, val_ref, count_ref, pick_ref, fblk_ref, ablk_ref, agg_ref, out_ref, inc_ref, inctab_ref,
    col_ref, pre_ref, mask_ref, score_ref, srow_ref, sout_ref, sin_ref, stab_ref, wsplit_ref, slot_ref,
    gout_ref, gin_ref, back_ref, dn_ref, dl_ref, acc_ref, dpre_ref, rs_out, rs_in, ag_ref, rs_mid, rs_got, wt_ref,
    feat_send, feat_recv, dom_send, dom_recv, load_sem,
):
    feat_ref, neigh_ref, degree_ref, send_ref, label_ref, ws_ref, wn_ref, bias_ref, as_ref, an_ref = held
    loads = [pltpu.make_async_copy(a, b, load_sem.at[k]) for k, (a, b) in enumerate(zip(inputs, held))]
    for k in (0, 3, 1, 2, 5, 7, 8, 9, 6, 4):
        loads[k].start()
    d = lax.axis_index("dom")
    f = lax.axis_index("feat")
    cols, nodes = feat_ref.shape
    fan = neigh_ref.shape[0]
    each = send_ref.shape[1]
    remote = parts * each
    table = nodes + remote
    block = nodes // slices
    hid = ws_ref.shape[1]
    rows = table // GROUPS
    shift = rows.bit_length() - 1

    chips = slices // 2
    chip, core = f // 2, lax.rem(f, 2)

    def feat_peer(j):
        return 2 * lax.rem(chip + j // 2, chips) + lax.rem(core + j % 2, 2)

    def feat_from(j):
        return 2 * lax.rem(chip + chips - j // 2, chips) + lax.rem(core + j % 2, 2)

    far_first = list(range(2, slices)) + [1]

    barrier = pltpu.get_barrier_semaphore()
    for j in range(1, parts):
        pl.semaphore_signal(barrier, inc=1, device_id={"dom": lax.rem(d + j, parts)}, device_id_type=MESH)
    for j in range(1, slices):
        pl.semaphore_signal(barrier, inc=1, device_id={"feat": feat_peer(j)}, device_id_type=MESH)

    sent = []

    def feat_copy(phase, j, src, dst):
        copy = pltpu.make_async_remote_copy(
            src_ref=src, dst_ref=dst, send_sem=feat_send.at[phase, j], recv_sem=feat_recv.at[phase, j],
            device_id={"feat": feat_peer(j)}, device_id_type=MESH)
        copy.start()
        sent.append(copy)

    def dom_copy(phase, j, src, dst):
        copy = pltpu.make_async_remote_copy(
            src_ref=src, dst_ref=dst, send_sem=dom_send.at[phase, j], recv_sem=dom_recv.at[phase, j],
            device_id={"dom": lax.rem(d + j, parts)}, device_id_type=MESH)
        copy.start()
        sent.append(copy)

    def forward(phase, j, src, dst):
        copy = pltpu.make_async_remote_copy(
            src_ref=src, dst_ref=dst, send_sem=feat_send.at[phase, j], recv_sem=feat_recv.at[phase, j],
            device_id={"feat": feat_peer(1)}, device_id_type=MESH)
        copy.start()
        sent.append(copy)

    def feat_wait(phase, j, dst):
        pltpu.make_async_remote_copy(
            src_ref=dst, dst_ref=dst, send_sem=feat_send.at[phase, j], recv_sem=feat_recv.at[phase, j],
            device_id={"feat": feat_peer(j)}, device_id_type=MESH).wait_recv()

    def dom_wait(phase, j, dst):
        pltpu.make_async_remote_copy(
            src_ref=dst, dst_ref=dst, send_sem=dom_send.at[phase, j], recv_sem=dom_recv.at[phase, j],
            device_id={"dom": lax.rem(d + j, parts)}, device_id_type=MESH).wait_recv()

    def dom_peer(j):
        return lax.rem(d + j, parts)

    def dom_from(j):
        return lax.rem(d + parts - j, parts)

    def span(index):
        return pl.ds(pl.multiple_of(index * block, block), block)

    loads[0].wait()
    loads[3].wait()

    def pick(i, _):
        r = pl.multiple_of(i * 256, 256)
        here = lax.broadcasted_iota(jnp.int32, (256, each), 0) + r
        for p in range(parts):
            pick_ref[pl.ds(r, 256), p * each:(p + 1) * each] = jnp.where(here == send_ref[p:p + 1, :], 1.0, 0.0).astype(BF)
        return 0

    lax.fori_loop(0, nodes // 256, pick, 0)
    step = min(256, remote)
    for c in range(remote // step):
        got = dot(feat_ref[...], pick_ref[:, c * step:(c + 1) * step], NN).astype(BF)
        for p in range(step // each):
            out_ref[c * (step // each) + p] = got[:, p * each:(p + 1) * each]
    pl.semaphore_wait(barrier, parts + slices - 2)
    cuts = 2 if cols % 32 == 0 else 1
    bands = [slice(c * cols // cuts, (c + 1) * cols // cuts) for c in range(cuts)]
    for c, band in enumerate(bands):
        for j in range(1, parts):
            dom_copy(7 * c, j, out_ref.at[dom_peer(j), band], inc_ref.at[d, band])
    inc_ref[d] = out_ref[d]

    for j in far_first:
        feat_copy(0, j, feat_ref.at[:, span(feat_peer(j))], fblk_ref.at[f])
    fblk_ref[f] = feat_ref[:, span(f)]

    loads[1].wait()
    loads[2].wait()
    slot = lax.broadcasted_iota(jnp.int32, (fan, nodes), 0)
    used = slot < degree_ref[...]
    hi_ref[...] = neigh_ref[...] & (rows - 1)
    val_ref[...] = jnp.where(used, jnp.left_shift(jnp.int32(1), (neigh_ref[...] >> shift) * BITS), 0)

    def count_lanes(c, first):
        lanes = pl.ds(pl.multiple_of(first + c * 128, 128), 128)
        his = [jnp.broadcast_to(hi_ref[k:k + 1, lanes], (8, 128)) for k in range(fan)]
        vals = [jnp.broadcast_to(val_ref[k:k + 1, lanes], (8, 128)) for k in range(fan)]
        base = lax.broadcasted_iota(jnp.int32, (8, 128), 0)

        def count_rows(i, _):
            for u in range(0, 64, 16):
                r = pl.multiple_of(i * 64 + u, 16)
                words = []
                for here in (base + r, base + (r + 8)):
                    terms = [jnp.where(h == here, v, 0) for h, v in zip(his, vals)]
                    while len(terms) > 1:
                        terms = [a + b for a, b in zip(terms[::2], terms[1::2])] + terms[len(terms) & ~1:]
                    words.append(terms[0])
                for g in range(GROUPS):
                    fields = [w >> (BITS * g) if g else w for w in words]
                    if g < GROUPS - 1:
                        fields = [w & ((1 << BITS) - 1) for w in fields]
                    both = jnp.concatenate([w.astype(F32) for w in fields], axis=0)
                    count_ref[pl.ds(pl.multiple_of(g * rows + r, 16), 16), lanes] = both.astype(BF)
            return 0

        lax.fori_loop(0, rows // 64, count_rows, 0)
        return first

    def count_block(index):
        lax.fori_loop(0, block // 128, count_lanes, index * block)

    far = far_first[:-1]
    for j in far:
        count_block(feat_peer(j))
    inverse = 1.0 / degree_ref[...].astype(F32)

    for k in (7, 8, 9):
        loads[k].wait()
    for k, ref in enumerate((bias_ref, as_ref, an_ref)):
        col_ref[k] = jnp.broadcast_to(ref[...], (128, hid)).T

    tile = min(256, block)

    def aggregate(index, band):
        for t in range(block // tile):
            lanes = pl.ds(pl.multiple_of(index * block + t * tile, tile), tile)
            sums = dot(feat_ref[band, :], count_ref[:nodes, lanes], NN)
            sums = sums + dot(inctab_ref[band, :], count_ref[nodes:, lanes], NN)
            agg_ref[band, lanes] = (sums * (1.0 / degree_ref[:, lanes].astype(F32))).astype(BF)

    for c, band in enumerate(bands):
        if c == cuts - 1:
            count_block(feat_peer(1))
        for j in range(1, parts):
            dom_wait(7 * c, j, inc_ref.at[dom_from(j), band])
        for p in range(parts):
            inctab_ref[band, p * each:(p + 1) * each] = inc_ref[p, band]
        for j in far:
            aggregate(feat_peer(j), band)
            feat_copy(1 + 3 * c, j, agg_ref.at[band, span(feat_peer(j))], ablk_ref.at[f, band])
    whole_band = slice(0, cols)
    aggregate(feat_peer(1), whole_band)
    feat_copy(1, 1, agg_ref.at[:, span(feat_peer(1))], ablk_ref.at[f])
    count_block(f)
    aggregate(f, whole_band)
    ablk_ref[f] = agg_ref[:, span(f)]

    for j in range(1, slices):
        feat_wait(0, j, fblk_ref.at[feat_from(j)])
    depth = slices * cols
    loads[5].wait()
    loads[6].wait()
    wt_ref[0] = ws_ref[...].T
    wt_ref[1] = wn_ref[...].T
    pre_ref[...] = dot(wt_ref[0], fblk_ref[...].reshape(depth, block), NN)
    feat_wait(1, 1, ablk_ref.at[feat_from(1)])
    for c, band in enumerate(bands):
        for j in far:
            feat_wait(1 + 3 * c, j, ablk_ref.at[feat_from(j), band])
    pre_ref[...] += dot(wt_ref[1], ablk_ref[...].reshape(depth, block), NN)
    for t in range(block // 128):
        pre = pre_ref[:, t * 128:(t + 1) * 128] + col_ref[0]
        hidden = jnp.maximum(pre, 0.0)
        mask_ref[f, :, t * 128:(t + 1) * 128] = jnp.where(pre > 0, 1.0, 0.0).astype(BF)
        own = jnp.broadcast_to(total(hidden * col_ref[1]), (8, 128))
        other = jnp.broadcast_to(total(hidden * col_ref[2]), (8, 128))
        sub = lax.broadcasted_iota(jnp.int32, (8, 128), 0)
        score_ref[f, :, t * 128:(t + 1) * 128] = jnp.where(sub == 0, own, other)
    for j in far_first:
        feat_copy(2, j, score_ref.at[f], score_ref.at[f])
    for j in range(2, slices, 2):
        feat_copy(3, j, mask_ref.at[f], mask_ref.at[f])
    feat_copy(3, 1, mask_ref.at[f], mask_ref.at[f])

    for j in range(1, slices):
        feat_wait(2, j, score_ref.at[feat_from(j)])
    for s in range(slices):
        srow_ref[:, s * block:(s + 1) * block] = score_ref[s]
    own_score = split(srow_ref[1:2, :])
    boundary = total(dot(own_score, pick_ref[...], NN))
    for p in range(parts):
        sout_ref[p] = jnp.broadcast_to(boundary[:, p * each:(p + 1) * each], (8, each))
    for j in range(1, parts):
        dom_copy(1, j, sout_ref.at[dom_peer(j)], sin_ref.at[d])
    sin_ref[d] = sout_ref[d]

    def own_tile(i):
        lanes = slice(i * 256, (i + 1) * 256)
        slot_ref[0:1, lanes] = total(dot(own_score, count_ref[:nodes, lanes], NN))

    for i in range(0, nodes // 256):
        own_tile(i)
    for j in range(1, parts):
        dom_wait(1, j, sin_ref.at[dom_from(j)])
    for p in range(parts):
        stab_ref[:, p * each:(p + 1) * each] = sin_ref[p]
    spread = split(stab_ref[0:1, :])

    def logit_tile(i):
        lanes = slice(i * 256, (i + 1) * 256)
        slot_ref[0:1, lanes] += total(dot(spread, count_ref[nodes:, lanes], NN))

    for i in range(0, nodes // 256):
        logit_tile(i)
    logits = srow_ref[0:1, :] + slot_ref[0:1, :nodes] * inverse
    logit_ref[...] = logits
    loads[4].wait()
    dlogit = (1.0 / (1.0 + jnp.exp(-logits)) - label_ref[...].astype(F32)) * scale
    dl_ref[...] = dlogit
    wsplit_ref[...] = split(dlogit * inverse)

    def slot_tile(i):
        lanes = slice(i * 256, (i + 1) * 256)
        slot_ref[0:1, lanes] = total(dot(wsplit_ref[...], count_ref[lanes, :], NT))

    for i in range(nodes // 256, table // 256):
        slot_tile(i)
    for p in range(parts):
        gout_ref[p] = jnp.broadcast_to(slot_ref[0:1, nodes + p * each:nodes + (p + 1) * each], (8, each))
    for j in range(1, parts):
        dom_copy(2, j, gout_ref.at[dom_peer(j)], gin_ref.at[d])
    gin_ref[d] = gout_ref[d]
    for i in range(0, nodes // 256):
        slot_tile(i)

    for j in range(2, slices, 2):
        feat_wait(3, j, mask_ref.at[feat_from(j)])
        index = feat_from(j)
        forward(3, j + 1, mask_ref.at[index], mask_ref.at[index])

    for j in range(1, parts):
        dom_wait(2, j, gin_ref.at[dom_from(j)])
    for p in range(parts):
        back_ref[:, p * each:(p + 1) * each] = gin_ref[p]
    returned = split(back_ref[0:1, :])

    def back_tile(i):
        lanes = slice(i * 256, (i + 1) * 256)
        dn_ref[0:1, lanes] = slot_ref[0:1, lanes] + total(dot(returned, pick_ref[lanes, :], NT))

    for i in range(0, nodes // 256):
        back_tile(i)

    for j in range(slices):
        index = feat_from(j)
        if j % 2:
            feat_wait(3, j, mask_ref.at[index])
        for t in range(block // 128):
            lanes = pl.ds(pl.multiple_of(index * block + t * 128, 128), 128)
            grad = dl_ref[:, lanes] * col_ref[1] + dn_ref[0:1, lanes] * col_ref[2]
            dpre_ref[j, :, t * 128:(t + 1) * 128] = grad.astype(BF) * mask_ref[index, :, t * 128:(t + 1) * 128]
        own = dot(feat_ref[:, span(index)], dpre_ref[j], NT)
        acc_ref[0] = acc_ref[0] + own if j else own

    half = hid // 2
    share = 2 * cols // parts
    spots = [(slice(p // 2 * share, (p // 2 + 1) * share), slice(p % 2 * half, (p % 2 + 1) * half)) for p in range(parts)]

    beside = d + 1 - 2 * lax.rem(d, 2)

    def to_beside(phase, j, src, dst):
        copy = pltpu.make_async_remote_copy(
            src_ref=src, dst_ref=dst, send_sem=dom_send.at[phase, j], recv_sem=dom_recv.at[phase, j],
            device_id={"dom": beside}, device_id_type=MESH)
        copy.start()
        sent.append(copy)

    def send_shares(h):
        for p in range(parts):
            rs_out[h, p] = acc_ref[h, spots[p][0], spots[p][1]].astype(BF)
        for j in list(range(2, parts, 2)) + [0]:
            index = lax.rem(beside + j, parts)
            to_beside(3 + h, j + 1, rs_out.at[h, index], rs_in.at[h, index])

    if reduce_here:
        send_shares(0)
    for j in range(slices):
        other = dot(agg_ref[:, span(feat_from(j))], dpre_ref[j], NT)
        acc_ref[1] = acc_ref[1] + other if j else other
    if reduce_here:
        send_shares(1)
        for h in range(2):
            for j in range(2, parts, 2):
                index = dom_peer(j)
                dom_wait(3 + h, j + 1, rs_in.at[h, index])
                pair = rs_out[h, index].astype(F32) + rs_in[h, index].astype(F32)
                rs_mid[h, index] = pair.astype(BF)
                dom_copy(3 + h, j, rs_mid.at[h, index], rs_got.at[h, d])
        for h in range(2):
            dom_wait(3 + h, 1, rs_in.at[h, d])
            whole = rs_out[h, d].astype(F32) + rs_in[h, d].astype(F32)
            for j in range(2, parts, 2):
                dom_wait(3 + h, j, rs_got.at[h, dom_from(j)])
                whole = whole + rs_got[h, dom_from(j)].astype(F32)
            ag_ref[h, d] = whole.astype(BF)
            for j in range(2, parts, 2):
                dom_copy(5 + h, j, ag_ref.at[h, d], ag_ref.at[h, d])
            to_beside(5 + h, 1, ag_ref.at[h, d], ag_ref.at[h, d])
        for h in range(2):
            for j in range(2, parts, 2):
                dom_wait(5 + h, j, ag_ref.at[h, dom_from(j)])
                to_beside(5 + h, j + 1, ag_ref.at[h, dom_from(j)], ag_ref.at[h, dom_from(j)])
        for h, ref in enumerate((gself_ref, gneigh_ref)):
            for j in range(1, parts, 2):
                dom_wait(5 + h, j, ag_ref.at[h, lax.rem(beside + parts + 1 - j, parts)])
            for p in range(parts):
                ref[spots[p][0], spots[p][1]] = ag_ref[h, p]
    else:
        gself_ref[...] = acc_ref[0]
        gneigh_ref[...] = acc_ref[1]
    for copy in sent:
        copy.wait_send()


def place(logit_ref, gself_ref, gneigh_ref, logit_out, gself_out, gneigh_out):
    logit_out[...] = logit_ref[...]
    gself_out[...] = gself_ref[...].astype(F32)
    gneigh_out[...] = gneigh_ref[...].astype(F32)


def body(features, neighbors, degree, send_rows, labels, w_self, w_neigh, bias, a_self, a_neigh):
    parts = lax.axis_size("dom")
    slices = lax.axis_size("feat")
    cols, nodes = features.shape
    fan = neighbors.shape[0]
    each = send_rows.shape[2]
    remote = parts * each
    table = nodes + remote
    block = nodes // slices
    hid = w_self.shape[1]
    share = 2 * cols // parts
    reduce_here = parts % 2 == 0 and share * parts == 2 * cols and share % 16 == 0 and hid % 256 == 0
    scale = float(nodes * parts) ** (-0.5)
    spare = share if reduce_here else 16
    V = pltpu.VMEM
    held = [
        V((cols, nodes), BF), V((fan, nodes), jnp.int32), V((1, nodes), jnp.int32), V((parts, each), jnp.int32),
        V((1, nodes), jnp.int32), V(w_self.shape, BF), V(w_neigh.shape, BF),
        V((1, hid), F32), V((1, hid), F32), V((1, hid), F32),
    ]
    scratch = held + [
        V((fan, nodes), jnp.int32), V((fan, nodes), jnp.int32),
        V((table, nodes), BF), V((nodes, remote), BF),
        V((slices, cols, block), BF), V((slices, cols, block), BF), V((cols, nodes), BF),
        V((parts, cols, each), BF), V((parts, cols, each), BF), V((cols, remote), BF),
        V((3, hid, 128), F32), V((hid, block), F32), V((slices, hid, block), BF),
        V((slices, 8, block), F32), V((8, nodes), F32),
        V((parts, 8, each), F32), V((parts, 8, each), F32), V((8, remote), F32),
        V((16, nodes), BF), V((8, table), F32),
        V((parts, 8, each), F32), V((parts, 8, each), F32), V((8, remote), F32),
        V((8, nodes), F32), V((1, nodes), F32),
        V((2, cols, hid), F32), V((slices, hid, block), BF),
        *[V((2, parts, spare, hid // 2), BF)] * 5,
        V((2, hid, w_self.shape[0]), BF),
        pltpu.SemaphoreType.DMA((5, slices)), pltpu.SemaphoreType.DMA((5, slices)),
        pltpu.SemaphoreType.DMA((8, parts)), pltpu.SemaphoreType.DMA((8, parts)),
        pltpu.SemaphoreType.DMA((10,)),
    ]
    vm = pl.BlockSpec(memory_space=pltpu.VMEM)
    logits, grad_self, grad_neigh = pl.pallas_call(
        functools.partial(kernel, parts, slices, reduce_here, scale),
        out_shape=(
            jax.ShapeDtypeStruct((1, nodes), F32),
            jax.ShapeDtypeStruct((cols, hid), BF if reduce_here else F32),
            jax.ShapeDtypeStruct((cols, hid), BF if reduce_here else F32),
        ),
        in_specs=[pl.BlockSpec(memory_space=pltpu.HBM)] * 10,
        out_specs=(vm, vm, vm),
        scratch_shapes=scratch,
        compiler_params=pltpu.CompilerParams(
            collective_id=0, has_side_effects=True, vmem_limit_bytes=62 * 1024 * 1024),
    )(
        features, neighbors, degree.reshape(1, nodes), send_rows.reshape(parts, each), labels.reshape(1, nodes),
        w_self, w_neigh, bias.reshape(1, hid), a_self.reshape(1, hid), a_neigh.reshape(1, hid),
    )
    if reduce_here:
        logits, grad_self, grad_neigh = pl.pallas_call(
            place,
            out_shape=tuple(jax.ShapeDtypeStruct(x.shape, F32) for x in (logits, grad_self, grad_neigh)),
            in_specs=[vm] * 3,
            out_specs=(vm, vm, vm),
            compiler_params=pltpu.CompilerParams(vmem_limit_bytes=62 * 1024 * 1024),
        )(logits, grad_self, grad_neigh)
    else:
        grad_self, grad_neigh = lax.psum((grad_self, grad_neigh), "dom")
    return (logits.reshape(nodes), grad_self, grad_neigh)


def solution(mesh):
    return jax.shard_map(
        body,
        mesh=mesh,
        in_specs=(
            P("feat", "dom"), P(None, "dom"), P("dom"), P("dom", None, None), P("dom"),
            P(), P(), P(), P(), P(),
        ),
        out_specs=(P("dom"), P("feat", None), P("feat", None)),
        check_vma=False,
    )
```
